512 devices in a mesh: lat: 32 (over z, core), lev: 16 (over y, x).
Axes of the slice: x: 4, y: 4, z: 16, core: 2. Of those that a mesh axis runs over, the one named last changes fastest.
Arguments:
- obs_band: int32 [131072, 1], P('lat'), may hold values from 0 to 31; in each aligned block of 4096 rows (0 to 4095, 4096 to 8191, ...) at most 384 rows name the same one
- obs_cell: int32 [131072], P('lat'), may hold values from 0 to 63487
- obs_weight: bfloat16 [131072, 4], P('lat'), may hold values from 0.099609375 to 1
- obs_profile: bfloat16 [131072, 128], P('lat', 'lev'), may hold values from -0.59765625 to 0.59765625
- legendre_table: bfloat16 [512, 1025, 1024], P(('lat', 'lev')), may hold values from -0.1875 to 0.1875
- covariance_root: bfloat16 [4, 1024, 32, 32], P(None, 'lev'), may hold values from -1 to 1
Outputs:
- control_gradient: bfloat16 [1024, 1024, 2, 128], P('lat', 'lev')
The draws below stay inside these ranges and needn't reach their ends.
Inputs may be any that keep to these rules, and one draw needn't show every extreme that they name: `obs_band`: in the rows of one lat index at most 384 name the same band, a bound that some block reaches of them.
All inputs are finite; a program needn't handle non-finite values.
Results may differ from the reference program's by a relative error of at most 0.0058.
Values may be sent and summed in bfloat16 or wider, within the bound.
A program may use at most 192 MiB of HBM per device.

```python
import math
import jax
import jax.numpy as jnp
import numpy as np
from jax import lax

FIELDS = 4
LEVELS = 32
CH = 128
NLAT = 1024
NLON = 2048
M = 1024
LATB = 32
OBS_DEV = 4096
OBS = 131072
CAP = 384
N_LAT = 32


def plant(values, stream_key, smallest, high):
    extent = values.shape
    place = [jax.random.randint(jax.random.fold_in(stream_key, axis), (), 0, extent[axis]) for axis in range(len(extent))]
    values = values.at[tuple(place)].set(smallest)
    longest = extent.index(max(extent))
    place[longest] = (place[longest] + 1) % extent[longest]
    return values.at[tuple(place)].set(high)


def block_scale(key, dims, cuts, smallest, top_value):
    def one(axis_at, parts):
        heights = jax.random.uniform(jax.random.fold_in(jax.random.fold_in(key, 6), axis_at), (parts,), jnp.float32, smallest / len(cuts), top_value / len(cuts))
        return jnp.repeat(jnp.exp(heights), dims[axis_at] // parts).reshape((-1,) + (1,) * (len(dims) - axis_at - 1))

    gain = one(*cuts[0])
    for cut in cuts[1:]:
        gain = gain * one(*cut)
    return gain


def shared_out(stream_key, own, number, rows, count, top, limit, skew):
    sequence = jax.random.permutation(stream_key, count)
    packed, ordinary = shares(count, rows * top, limit, skew, True), shares(count, rows * top, limit, skew, False)
    places = jnp.arange(count)

    def named(sizes, rotation):
        used = int((sizes > 0).sum())
        fixed = max(1, used // 4)
        passed = fixed + (places - fixed + rotation * (used - fixed)) % max(1, count - fixed)
        return jnp.zeros((count,), jnp.int32).at[sequence[jnp.where(places < fixed, places, passed)]].set(jnp.asarray(sizes, jnp.int32))

    sizes = jnp.where(number % 4 == 0, named(packed, number // 4), named(ordinary, number - number // 4 - 1))
    mixed = jax.random.permutation(jax.random.fold_in(own, 3), count)
    source_of, sink = mixed[0:count // 2 * 2:2], mixed[1:count // 2 * 2:2]
    room = jnp.minimum(sizes[source_of] - 1, limit - sizes[sink]) // 2
    room = jnp.where((source_of == sequence[0]) | (sink == sequence[0]) | (sizes[sink] == 0), 0, jnp.maximum(room, 0))
    passed = jax.random.randint(jax.random.fold_in(own, 4), (count // 2,), 0, 1 << 20) % (room + 1)
    sizes = sizes.at[source_of].add(-passed).at[sink].add(passed)
    items = jnp.searchsorted(jnp.cumsum(sizes), jnp.arange(rows * top), side="right").astype(jnp.int32)
    grid = items.reshape(top, rows).T
    grid = grid[jax.random.permutation(jax.random.fold_in(own, 1), rows)]
    rotation = jax.random.randint(jax.random.fold_in(own, 2), (rows, 1), 0, top)
    return jnp.take_along_axis(grid, (jnp.arange(top)[None, :] + rotation) % top, axis=1)


def shares(amount, total, limit, slope, full):
    portions = [(1 << 20) // math.isqrt(standing ** slope) + 1 for standing in range(1, amount + 1)]
    largest = limit if full else min(limit, max(-(-total // amount), total * portions[0] // sum(portions)))
    least = 1 if total - largest >= amount - 1 else 0
    given, rest = [largest] + [least] * (amount - 1), total - largest - least * (amount - 1)
    while rest > 0:
        candidates = [i for i in range(1, amount) if given[i] < largest] or [i for i in range(1, amount) if given[i] < limit]
        mass, left = sum([portions[i] for i in candidates]), rest
        for i in candidates:
            extra = min(limit - given[i], max(1, left * portions[i] // mass), rest)
            given[i] = given[i] + extra
            rest = rest - extra
    return np.array(given)


def scatter_about(stream_key, extent, width, reach, shards=(), kind=jnp.bfloat16):
    factor_of = block_scale(stream_key, extent, shards, -0.22, 0.18) if shards else 1.0
    array = jax.random.normal(stream_key, extent, jnp.float32) * width * factor_of
    return jnp.minimum(jnp.maximum(array, -reach), reach).astype(kind)


def setup_inputs(seed: int = 0) -> dict:
    keys = jax.random.split(jax.random.key(seed), 7)
    obs_band_keys = jax.random.split(jax.random.fold_in(keys[0], 1), OBS // OBS_DEV)
    obs_band_turns = jax.random.permutation(jax.random.fold_in(keys[0], 3), OBS // OBS_DEV)
    obs_band = jax.vmap(lambda own, number: shared_out(jax.random.fold_in(keys[0], 2), own, number, OBS_DEV, N_LAT, 1, CAP, 2))(obs_band_keys, obs_band_turns).reshape((OBS, 1))
    obs_cell = plant(jax.random.randint(keys[1], (OBS,), 0, (LATB - 1) * NLON), jax.random.fold_in(keys[1], 1), 0, ((LATB - 1) * NLON) - 1).astype(jnp.int32)
    obs_weight = jnp.clip(0.099609375 + 0.9003906 * jax.random.uniform(keys[2], (OBS, 4), jnp.float32) ** block_scale(keys[2], (OBS, 4), ((0, 32),), -0.2, 0.2), 0.099609375, 1.0).astype(jnp.bfloat16)
    obs_profile = scatter_about(keys[3], (OBS, CH), 0.1, 0.59765625, ((0, 32), (1, 16)))
    legendre_table = scatter_about(keys[4], (M // 2, M + 1, NLAT), NLAT ** -0.5, 0.1875, ((0, 512),))
    covariance_root = scatter_about(keys[5], (FIELDS, M, LEVELS, LEVELS), LEVELS ** -0.5, 1.0, ((1, 16),))
    return {"obs_band": obs_band, "obs_cell": obs_cell, "obs_weight": obs_weight, "obs_profile": obs_profile, "legendre_table": legendre_table, "covariance_root": covariance_root}


def pair_wavenumbers(total_count):
    slot_index = jnp.arange(total_count, dtype=jnp.int32)
    half_index = slot_index // 2
    return jnp.where(slot_index % 2 == 0, half_index, total_count - 1 - half_index)


def fourier_tables(wavenumbers, length):
    points = jnp.arange(length, dtype=jnp.int32)
    phase = (points[:, None] * wavenumbers[None, :]) % length
    angle = phase.astype(jnp.float32) * jnp.float32(2.0 * math.pi / length)
    return jnp.cos(angle), -jnp.sin(angle)


def observation_grid(obs_band, obs_cell, obs_weight, obs_profile):
    rows_band = NLAT // N_LAT
    owner_band = obs_band[:, 0]
    cell_row = obs_cell // NLON
    cell_lon = obs_cell % NLON
    lon_east = (cell_lon + 1) % NLON
    row_start = (owner_band * rows_band + cell_row) * NLON
    corner_list = [row_start + cell_lon, row_start + lon_east, row_start + NLON + cell_lon, row_start + NLON + lon_east]
    profile = obs_profile.astype(jnp.float32)
    weight = obs_weight.astype(jnp.float32)
    grid_field = jnp.zeros((CH, NLAT * NLON), jnp.float32)
    for corner in range(4):
        grid_field = grid_field.at[:, corner_list[corner]].add((weight[:, corner:corner + 1] * profile).T)
    return grid_field


def reference(obs_band, obs_cell, obs_weight, obs_profile, legendre_table, covariance_root):
    grid_field = observation_grid(obs_band, obs_cell, obs_weight, obs_profile)
    cosine, sine = fourier_tables(pair_wavenumbers(M), NLON)

    def transform_channel(channel_grid):
        plane = channel_grid.reshape(NLAT, NLON)
        real_part = jnp.dot(plane, cosine, precision=lax.Precision.HIGHEST, preferred_element_type=jnp.float32)
        imag_part = jnp.dot(plane, sine, precision=lax.Precision.HIGHEST, preferred_element_type=jnp.float32)
        return jnp.stack([real_part, imag_part]).astype(jnp.bfloat16)

    fourier = lax.map(transform_channel, grid_field)
    fourier = jnp.transpose(fourier, (3, 1, 0, 2)).reshape(M // 2, 4 * CH, NLAT)
    degree_ids = jnp.arange(M, dtype=jnp.int32)
    roots = covariance_root.astype(jnp.float32)

    def one_pair(inputs):
        table_rows, pair_fourier, pair_id = inputs
        full = jnp.dot(table_rows.astype(jnp.float32), pair_fourier.astype(jnp.float32).T, preferred_element_type=jnp.float32)
        first_part = full[:, :2 * CH]
        second_part = full[:, 2 * CH:]
        padded = jnp.concatenate([jnp.zeros((M, 2 * CH), jnp.float32), first_part[:M]], axis=0)
        spec_first = lax.dynamic_slice_in_dim(padded, (M - pair_id).astype(jnp.int32), M, 0)
        spec_second = jnp.where((degree_ids >= M - 1 - pair_id)[:, None], second_part[1:], jnp.float32(0.0))
        spectra = lax.optimization_barrier(jnp.stack([spec_first, spec_second]).astype(jnp.bfloat16))
        spectra = spectra.astype(jnp.float32).reshape(2, M, 2, FIELDS, LEVELS)
        result = jnp.einsum('qnrfk,fnkl->qnrfl', spectra, roots)
        return result.reshape(2, M, 2, CH).astype(jnp.bfloat16)

    pair_ids = jnp.arange(M // 2, dtype=jnp.int32)
    output = lax.map(one_pair, (legendre_table, fourier, pair_ids))
    return output.reshape(M, M, 2, CH)
```

```python
import functools
import math

import jax
import jax.numpy as jnp
import ml_dtypes
import numpy as np
from jax import lax
from jax.experimental import pallas as pl
from jax.experimental.pallas import tpu as pltpu
from jax.sharding import PartitionSpec as P

NLAT = 1024
NLON = 2048
DEGREES = 1024
LAT = 32
LEV = 16
CAP = 384
ROWS = 4096
FEAT = 16
F32 = jnp.float32
BF16 = jnp.bfloat16
MESH = pl.DeviceIdType.MESH
NT = (((1,), (1,)), ((), ()))


def vmem():
    return pl.BlockSpec(memory_space=pltpu.VMEM)


def anywhere():
    return pl.BlockSpec(memory_space=pl.ANY)


def iota(shape, axis):
    return lax.broadcasted_iota(jnp.int32, shape, axis)


def dft_tables():
    slots = np.arange(DEGREES)
    wave = np.where(slots % 2 == 0, slots // 2, DEGREES - 1 - slots // 2)
    phase = (wave[:, None] * np.arange(NLON)[None, :]) % NLON
    angle = phase * (2.0 * math.pi / NLON)
    table = np.stack([np.cos(angle), -np.sin(angle)], axis=1).reshape(2 * DEGREES, NLON)
    high = table.astype(ml_dtypes.bfloat16)
    low = (table - high.astype(np.float64)).astype(ml_dtypes.bfloat16)
    return np.stack([high, low])


def pack_kernel(band_ref, cell_ref, feat_ref, out_ref, acc_ref):
    width = 512
    earlier = (iota((128, 128), 0) < iota((128, 128), 1)).astype(F32).astype(BF16)
    acc_ref[...] = jnp.zeros_like(acc_ref)

    def step(index, counts):
        at = pl.multiple_of(index * width, width)
        band = band_ref[:, pl.ds(at, width)]
        cell = cell_ref[:, pl.ds(at, width)]
        feat = feat_ref[:, pl.ds(at, width)].astype(F32)
        one = (iota((LAT, width), 0) == band).astype(F32)
        ranks = []
        for part in range(width // 128):
            mine = one[:, part * 128 : (part + 1) * 128]
            before = jnp.dot(mine.astype(BF16), earlier, preferred_element_type=F32)
            ranks.append(jnp.sum(mine * (before + counts), axis=0, keepdims=True))
            counts = counts + jnp.sum(mine, axis=1, keepdims=True)
        rank = jnp.concatenate(ranks, axis=1).astype(jnp.int32)
        row = lax.shift_right_logical(cell, 11)
        high = lax.bitwise_and(lax.shift_right_logical(cell, 7), 15)
        low = lax.bitwise_and(cell, 127)
        extra = jnp.where(iota((4, width), 0) == 0, row, jnp.where(iota((4, width), 0) == 1, high, low))
        full = jnp.concatenate([feat, extra.astype(F32)], axis=0)
        pieces = [
            jnp.where(band == which, full, 0.0).astype(BF16) for which in range(LAT)
        ]
        left = jnp.concatenate(pieces, axis=0)
        right = jnp.where(iota((CAP, width), 0) == rank, 1.0, 0.0).astype(BF16)
        acc_ref[...] += lax.dot_general(left, right, NT, preferred_element_type=F32)
        return counts

    lax.fori_loop(0, ROWS // width, step, jnp.zeros((LAT, 1), F32))
    for which in range(LAT):
        out_ref[which] = acc_ref[which * FEAT : (which + 1) * FEAT, :].astype(BF16)


def pack(band, cell, feat):
    return pl.pallas_call(
        pack_kernel,
        out_shape=jax.ShapeDtypeStruct((LAT, FEAT, CAP), BF16),
        in_specs=[vmem()] * 3,
        out_specs=vmem(),
        scratch_shapes=[pltpu.VMEM((LAT * FEAT, CAP), F32)],
        compiler_params=pltpu.CompilerParams(vmem_limit_bytes=48 << 20),
        name="pack_rows",
    )(band, cell, feat)


def step_offset(step):
    half = (step + 1) // 2
    return lax.rem(jnp.where(lax.rem(step, 2) == 1, half, LAT - half), LAT)


def rows_kernel(src_ref, dst_ref, send_sem, recv_sem, own_sem):
    me = lax.axis_index("lat")
    barrier = pltpu.get_barrier_semaphore()

    def greet(step, _):
        pl.semaphore_signal(
            barrier, inc=1, device_id={"lat": lax.rem(me + step, LAT)}, device_id_type=MESH
        )
        return 0

    lax.fori_loop(1, LAT, greet, 0)
    pl.semaphore_wait(barrier, LAT - 1)
    own = pltpu.make_async_copy(src_ref.at[me], dst_ref.at[0], own_sem)
    own.start()

    def copy(step):
        target = lax.rem(me + step_offset(step), LAT)
        return pltpu.make_async_remote_copy(
            src_ref=src_ref.at[target],
            dst_ref=dst_ref.at[step],
            send_sem=send_sem.at[step],
            recv_sem=recv_sem.at[step],
            device_id={"lat": target},
            device_id_type=MESH,
        )

    def start(step, _):
        copy(step).start()
        return 0

    def finish(step, _):
        copy(step).wait()
        return 0

    lax.fori_loop(1, LAT, start, 0)
    own.wait()
    lax.fori_loop(1, LAT, finish, 0)


def exchange_rows(packed):
    return pl.pallas_call(
        rows_kernel,
        out_shape=jax.ShapeDtypeStruct((LAT, FEAT, CAP), BF16),
        in_specs=[vmem()],
        out_specs=vmem(),
        scratch_shapes=[
            pltpu.SemaphoreType.DMA((LAT,)),
            pltpu.SemaphoreType.DMA((LAT,)),
            pltpu.SemaphoreType.DMA,
        ],
        compiler_params=pltpu.CompilerParams(
            collective_id=0, has_side_effects=True, vmem_limit_bytes=32 << 20
        ),
        name="exchange_rows",
    )(packed)


def build_factors(block, lon_ref, col_ref):
    feat = block.astype(F32)
    row = feat[12:13].astype(jnp.int32)
    high = feat[13:14].astype(jnp.int32)
    low = feat[14:15].astype(jnp.int32)
    east = lax.bitwise_and(high + 1, 15)
    lane_low = iota((128, CAP), 0)
    first = iota((16, CAP), 0) == 0
    for half in range(2):
        west_weight = feat[8 + 2 * half : 9 + 2 * half]
        east_weight = feat[9 + 2 * half : 10 + 2 * half]
        inside = jnp.where(
            lane_low == low, west_weight, jnp.where(lane_low == low + 1, east_weight, 0.0)
        ).astype(BF16)
        across = jnp.where(jnp.logical_and(first, low == 127), east_weight, 0.0).astype(BF16)
        columns = pl.ds(half * CAP, CAP)
        for tile in range(NLON // 128):
            here = jnp.broadcast_to(jnp.where(high == tile, 1.0, 0.0), (16, CAP)).astype(BF16)
            there = jnp.broadcast_to(jnp.where(east == tile, 1.0, 0.0), (16, CAP)).astype(BF16)
            for part in range(8):
                piece = inside[part * 16 : (part + 1) * 16] * here
                if part == 0:
                    piece = piece + across * there
                lon_ref[pl.ds(tile * 128 + part * 16, 16), columns] = piece
        wanted = iota((LAT, CAP), 0) == row + half
        for channel in range(8):
            value = jnp.where(wanted, feat[channel : channel + 1], 0.0).astype(BF16)
            col_ref[pl.ds(channel * LAT, LAT), columns] = value


def band_kernel(
    recv_ref, table_ref, out_ref, lon0, lon1, col0, col1, grid_ref, parts_ref, table_vmem, sem
):
    fetch = pltpu.make_async_copy(table_ref, table_vmem, sem)
    fetch.start()
    grid_ref[...] = jnp.zeros_like(grid_ref)
    build_factors(recv_ref[0], lon0, col0)

    def add(lon_ref, col_ref):
        grid_ref[...] += lax.dot_general(lon_ref[...], col_ref[...], NT, preferred_element_type=F32)

    def step(index, _):
        build_factors(recv_ref[2 * index + 1], lon1, col1)
        add(lon0, col0)
        build_factors(recv_ref[lax.rem(2 * index + 2, LAT)], lon0, col0)
        add(lon1, col1)
        return 0

    lax.fori_loop(0, LAT // 2, step, 0)
    grid = grid_ref[...]
    grid_high = grid.astype(BF16)
    parts_ref[:, 0:256] = grid_high
    parts_ref[:, 256:512] = (grid - grid_high.astype(F32)).astype(BF16)
    fetch.wait()
    chunk = 512

    def transform(index, _):
        at = pl.multiple_of(index * chunk, chunk)
        both = jnp.dot(
            table_vmem[0, pl.ds(at, chunk), :], parts_ref[...], preferred_element_type=F32
        )
        rest = jnp.dot(
            table_vmem[1, pl.ds(at, chunk), :], parts_ref[:, 0:256], preferred_element_type=F32
        )
        total = both[:, 0:256] + both[:, 256:512] + rest
        pairs = pl.ds(pl.multiple_of(index * (chunk // 4), chunk // 4), chunk // 4)
        west = total[:, 0:128].reshape(chunk // 4, 4, 128)
        east = total[:, 128:256].reshape(chunk // 4, 4, 128)
        out_ref[pairs, :, :] = jnp.concatenate([west, east], axis=1).astype(BF16)
        return 0

    lax.fori_loop(0, 2 * DEGREES // chunk, transform, 0)


def band_transform(received, table):
    return pl.pallas_call(
        band_kernel,
        out_shape=jax.ShapeDtypeStruct((DEGREES // 2, 8, 128), BF16),
        in_specs=[vmem(), anywhere()],
        out_specs=vmem(),
        scratch_shapes=[
            pltpu.VMEM((NLON, 2 * CAP), BF16),
            pltpu.VMEM((NLON, 2 * CAP), BF16),
            pltpu.VMEM((256, 2 * CAP), BF16),
            pltpu.VMEM((256, 2 * CAP), BF16),
            pltpu.VMEM((NLON, 256), F32),
            pltpu.VMEM((NLON, 512), BF16),
            pltpu.VMEM((2, 2 * DEGREES, NLON), BF16),
            pltpu.SemaphoreType.DMA,
        ],
        compiler_params=pltpu.CompilerParams(vmem_limit_bytes=60 << 20),
        name="band_transform",
    )(received, table)


GROUP = 8


def fourier_kernel(
    src_ref, dst_ref, mid_ref, z_send, z_recv, p_send, p_recv, own_sem
):
    me = lax.axis_index("lat")
    lev = lax.axis_index("lev")
    barrier = pltpu.get_barrier_semaphore()

    def greet_lat(step, _):
        pl.semaphore_signal(
            barrier, inc=1, device_id={"lat": lax.rem(me + step, LAT)}, device_id_type=MESH
        )
        return 0

    def greet_lev(step, _):
        pl.semaphore_signal(
            barrier, inc=1, device_id={"lev": lax.rem(lev + step, LEV)}, device_id_type=MESH
        )
        return 0

    lax.fori_loop(1, LAT, greet_lat, 0)
    lax.fori_loop(1, LEV, greet_lev, 0)
    pl.semaphore_wait(barrier, LAT + LEV - 2)

    def along_lat(step):
        target = lax.rem(me + step_offset(step), LAT)
        return pltpu.make_async_remote_copy(
            src_ref=src_ref.at[target],
            dst_ref=mid_ref.at[step],
            send_sem=z_send.at[step],
            recv_sem=z_recv.at[step],
            device_id={"lat": target},
            device_id_type=MESH,
        )

    def along_lev(group, step):
        target = lax.rem(lev + step, LEV)
        steps = pl.ds(group * GROUP, GROUP)
        return pltpu.make_async_remote_copy(
            src_ref=mid_ref.at[steps, target],
            dst_ref=dst_ref.at[steps, lev],
            send_sem=p_send.at[group, step],
            recv_sem=p_recv.at[group, step],
            device_id={"lev": target},
            device_id_type=MESH,
        )

    def start_lat(step, _):
        along_lat(step).start()
        return 0

    own = pltpu.make_async_copy(src_ref.at[me], mid_ref.at[0], own_sem.at[0])
    own.start()
    lax.fori_loop(1, LAT, start_lat, 0)
    own.wait()

    def forward(group, _):
        def arrive(step, _):
            along_lat(step).wait_recv()
            return 0

        lax.fori_loop(jnp.maximum(group * GROUP, 1), (group + 1) * GROUP, arrive, 0)

        def start_lev(step, _):
            along_lev(group, step).start()
            return 0

        lax.fori_loop(1, LEV, start_lev, 0)
        steps = pl.ds(group * GROUP, GROUP)
        keep = pltpu.make_async_copy(mid_ref.at[steps, lev], dst_ref.at[steps, lev], own_sem.at[1])
        keep.start()
        keep.wait()
        return 0

    lax.fori_loop(0, LAT // GROUP, forward, 0)

    def sent(step, _):
        along_lat(step).wait_send()
        return 0

    lax.fori_loop(1, LAT, sent, 0)

    def finish(group, _):
        def one(step, _):
            along_lev(group, step).wait()
            return 0

        lax.fori_loop(1, LEV, one, 0)
        return 0

    lax.fori_loop(0, LAT // GROUP, finish, 0)


def exchange_fourier(fourier):
    return pl.pallas_call(
        fourier_kernel,
        out_shape=jax.ShapeDtypeStruct((LAT, LEV, 8, 128), BF16),
        in_specs=[vmem()],
        out_specs=vmem(),
        scratch_shapes=[
            pltpu.VMEM((LAT, LEV, 8, 128), BF16),
            pltpu.SemaphoreType.DMA((LAT,)),
            pltpu.SemaphoreType.DMA((LAT,)),
            pltpu.SemaphoreType.DMA((LAT // GROUP, LEV)),
            pltpu.SemaphoreType.DMA((LAT // GROUP, LEV)),
            pltpu.SemaphoreType.DMA((2,)),
        ],
        compiler_params=pltpu.CompilerParams(
            collective_id=1, has_side_effects=True, vmem_limit_bytes=32 << 20
        ),
        name="exchange_fourier",
    )(fourier)


def legendre_kernel(
    place_ref, recv_ref, table_ref, out_ref, wide_ref, order_ref, pencil_ref, first_ref, second_ref
):
    me = place_ref[0]
    pair = place_ref[1]
    lane = iota((128, 128), 1)
    odd = lax.bitwise_and(lane, 32) != 0
    upper = lane >= 64

    for high in range(8):
        held = []
        for low in range(4):
            offset = lax.rem(me - (high * 4 + low) + LAT, LAT)
            step = jnp.where(offset == 0, 0, jnp.where(offset <= 16, 2 * offset - 1, 2 * (LAT - offset)))
            held.append(recv_ref[step].reshape(128, 128).astype(F32))
        mixed = [
            jnp.where(odd, pltpu.roll(held[1], 32, 1), held[0]),
            jnp.where(odd, held[1], pltpu.roll(held[0], 96, 1)),
            jnp.where(odd, pltpu.roll(held[3], 32, 1), held[2]),
            jnp.where(odd, held[3], pltpu.roll(held[2], 96, 1)),
        ]
        done = [
            jnp.where(upper, pltpu.roll(mixed[2], 64, 1), mixed[0]),
            jnp.where(upper, pltpu.roll(mixed[3], 64, 1), mixed[1]),
            jnp.where(upper, mixed[2], pltpu.roll(mixed[0], 64, 1)),
            jnp.where(upper, mixed[3], pltpu.roll(mixed[1], 64, 1)),
        ]
        for low in range(4):
            wide_ref[low] = done[low]
        for low in range(4):
            for which in range(4):
                order_ref[pl.ds(which * 128 + low, 32, stride=4), :] = wide_ref[
                    low, pl.ds(which, 32, stride=4), :
                ]
        pencil_ref[:, high * 128 : (high + 1) * 128] = order_ref[...].astype(BF16)

    first_ref[0:DEGREES] = jnp.zeros((DEGREES, 256), F32)
    chunk = 512
    for start in range(0, DEGREES, chunk):
        rows = table_ref[start : start + chunk, :]
        first_ref[DEGREES + start : DEGREES + start + chunk] = lax.dot_general(
            rows, pencil_ref[0:256], NT, preferred_element_type=F32
        )
        second_ref[start : start + chunk] = lax.dot_general(
            rows, pencil_ref[256:512], NT, preferred_element_type=F32
        )
    second_ref[DEGREES : DEGREES + 1] = lax.dot_general(
        table_ref[DEGREES : DEGREES + 1, :], pencil_ref[256:512], NT, preferred_element_type=F32
    )
    degree = iota((64, 256), 0)
    for block in range(16):
        start = pl.multiple_of(DEGREES + block * 64 - (pair + 7) // 8 * 8, 8)
        window = first_ref[pl.ds(start, 72), :]
        skip = lax.rem(8 - lax.rem(pair, 8), 8)
        out_ref[block, 0] = pltpu.roll(window, lax.rem(72 - skip, 72), 0)[0:64].astype(BF16)
        moved = second_ref[block * 64 + 1 : block * 64 + 65, :]
        keep = degree >= DEGREES - 1 - pair - block * 64
        out_ref[block, 1] = jnp.where(keep, moved, 0.0).astype(BF16)


def legendre(place, received, table):
    return pl.pallas_call(
        legendre_kernel,
        out_shape=jax.ShapeDtypeStruct((LEV, 2, 64, 256), BF16),
        in_specs=[pl.BlockSpec(memory_space=pltpu.SMEM), vmem(), vmem()],
        out_specs=vmem(),
        scratch_shapes=[
            pltpu.VMEM((4, 128, 128), F32),
            pltpu.VMEM((512, 128), F32),
            pltpu.VMEM((512, NLAT), BF16),
            pltpu.VMEM((2 * DEGREES + 8, 256), F32),
            pltpu.VMEM((DEGREES + 8, 256), F32),
        ],
        compiler_params=pltpu.CompilerParams(vmem_limit_bytes=48 << 20),
        name="legendre",
    )(place, received, table)


def spectra_kernel(src_ref, dst_ref, send_sem, recv_sem, own_sem):
    me = lax.axis_index("lat")
    lev = lax.axis_index("lev")
    begin = [me // 4, LEV - 1 - me // 4]
    barrier = pltpu.get_barrier_semaphore()

    def greet(step, _):
        pl.semaphore_signal(
            barrier, inc=1, device_id={"lev": lax.rem(lev + step, LEV)}, device_id_type=MESH
        )
        return 0

    lax.fori_loop(1, LEV, greet, 0)
    pl.semaphore_wait(barrier, LEV - 1)

    def copy(step, slot):
        target = lax.rem(lev + step, LEV)
        return target, pltpu.make_async_remote_copy(
            src_ref=src_ref.at[target, slot],
            dst_ref=dst_ref.at[lev, slot],
            send_sem=send_sem.at[slot, step],
            recv_sem=recv_sem.at[slot, step],
            device_id={"lev": target},
            device_id_type=MESH,
        )

    def start(step, _):
        for slot in range(2):
            target, moving = copy(step, slot)

            @pl.when(target >= begin[slot])
            def _():
                moving.start()

        return 0

    lax.fori_loop(1, LEV, start, 0)
    own = pltpu.make_async_copy(src_ref.at[lev], dst_ref.at[lev], own_sem)
    own.start()

    def clear(step, _):
        source = lax.rem(lev + step, LEV)
        for slot in range(2):

            @pl.when(lev < begin[slot])
            def _():
                dst_ref[source, slot] = jnp.zeros((64, 256), BF16)

        return 0

    lax.fori_loop(1, LEV, clear, 0)
    own.wait()

    def finish(step, _):
        for slot in range(2):
            target, moving = copy(step, slot)

            @pl.when(target >= begin[slot])
            def _():
                moving.wait_send()

            @pl.when(lev >= begin[slot])
            def _():
                moving.wait_recv()

        return 0

    lax.fori_loop(1, LEV, finish, 0)


def exchange_spectra(spectra):
    return pl.pallas_call(
        spectra_kernel,
        out_shape=jax.ShapeDtypeStruct((LEV, 2, 64, 256), BF16),
        in_specs=[vmem()],
        out_specs=vmem(),
        scratch_shapes=[
            pltpu.SemaphoreType.DMA((2, LEV)),
            pltpu.SemaphoreType.DMA((2, LEV)),
            pltpu.SemaphoreType.DMA,
        ],
        compiler_params=pltpu.CompilerParams(
            collective_id=2, has_side_effects=True, vmem_limit_bytes=32 << 20
        ),
        name="exchange_spectra",
    )(spectra)


def roots_kernel(spec_ref, root_ref, out_ref, block_ref, wide_ref):
    spread = (iota((32, 128), 0) == lax.bitwise_and(iota((32, 128), 1), 31)).astype(F32).astype(BF16)
    group = lax.shift_right_logical(iota((2048, 128), 1), 5)
    for field in range(4):
        copies = jnp.dot(
            root_ref[field].reshape(2048, 32), spread, preferred_element_type=F32
        )
        block_ref[:, field * 32 : (field + 1) * 32, :] = (
            jnp.where(group == field, copies, 0.0).astype(BF16).reshape(64, 32, 128)
        )
    for row in range(32):
        block = spec_ref[row // 2, row % 2].astype(F32)
        for part in range(2):
            wide_ref[part, row * 64 : (row + 1) * 64, :] = block[:, part * 128 : (part + 1) * 128]

    def step(degree, _):
        rows = pl.ds(degree, 32, stride=64)
        both = jnp.concatenate([wide_ref[0, rows, :], wide_ref[1, rows, :]], axis=0).astype(BF16)
        made = jnp.dot(both, block_ref[degree], preferred_element_type=F32)
        wide_ref[0, rows, :] = made[0:32]
        wide_ref[1, rows, :] = made[32:64]
        return 0

    lax.fori_loop(0, 64, step, 0, unroll=4)
    for part in range(2):
        out_ref[:, part * 128 : (part + 1) * 128] = wide_ref[part].astype(BF16)


def apply_roots(blocks, roots):
    return pl.pallas_call(
        roots_kernel,
        out_shape=jax.ShapeDtypeStruct((2048, 256), BF16),
        in_specs=[vmem(), vmem()],
        out_specs=vmem(),
        scratch_shapes=[
            pltpu.VMEM((64, 128, 128), BF16),
            pltpu.VMEM((2, 2048, 128), F32),
        ],
        compiler_params=pltpu.CompilerParams(vmem_limit_bytes=48 << 20),
        name="apply_roots",
    )(blocks, roots)


def on_device(table, obs_band, obs_cell, obs_weight, obs_profile, legendre_table, covariance_root):
    lat_index = lax.axis_index("lat")
    lev_index = lax.axis_index("lev")
    feat = jnp.concatenate([obs_profile.T, obs_weight.T], axis=0)
    packed = pack(obs_band.reshape(1, ROWS), obs_cell.reshape(1, ROWS), feat)
    received = exchange_rows(packed)
    fourier = band_transform(received, table)
    pencils = exchange_fourier(fourier.reshape(LAT, LEV, 8, 128))
    place = jnp.stack([lat_index, lat_index * LEV + lev_index]).astype(jnp.int32)
    spectra = legendre(place, pencils, legendre_table.reshape(DEGREES + 1, NLAT))
    blocks = exchange_spectra(spectra)
    return apply_roots(blocks, covariance_root).reshape(2 * LEV, 64, 2, 128)


def solution(mesh):
    in_specs = (
        P("lat", None),
        P("lat"),
        P("lat", None),
        P("lat", "lev"),
        P(("lat", "lev"), None, None),
        P(None, "lev", None, None),
    )
    out_specs = P("lat", "lev", None, None)
    table = dft_tables()

    def program(*args):
        return jax.shard_map(
            lambda *inner: on_device(jnp.asarray(table), *inner),
            mesh=mesh,
            in_specs=in_specs,
            out_specs=out_specs,
            check_vma=False,
        )(*args)

    return program
```

```python
import math

import jax
import jax.numpy as jnp
import ml_dtypes
import numpy as np
from jax import lax
from jax.experimental import pallas as pl
from jax.experimental.pallas import tpu as pltpu
from jax.sharding import PartitionSpec as P

NLAT = 1024
NLON = 2048
DEGREES = 1024
LAT = 32
LEV = 16
CAP = 384
ROWS = 4096
FEAT = 16
F32 = jnp.float32
BF16 = jnp.bfloat16
MESH = pl.DeviceIdType.MESH
NT = (((1,), (1,)), ((), ()))


def vmem():
    return pl.BlockSpec(memory_space=pltpu.VMEM)


def anywhere():
    return pl.BlockSpec(memory_space=pl.ANY)


def iota(shape, axis):
    return lax.broadcasted_iota(jnp.int32, shape, axis)


def dft_tables():
    slots = np.arange(DEGREES)
    wave = np.where(slots % 2 == 0, slots // 2, DEGREES - 1 - slots // 2)
    phase = (wave[:, None] * np.arange(NLON)[None, :]) % NLON
    angle = phase * (2.0 * math.pi / NLON)
    table = np.stack([np.cos(angle), -np.sin(angle)], axis=1).reshape(2 * DEGREES, NLON)
    high = table.astype(ml_dtypes.bfloat16)
    low = (table - high.astype(np.float64)).astype(ml_dtypes.bfloat16)
    return np.stack([high, low])


def pack_rows(band_ref, cell_ref, feat_ref, out_ref, acc_ref):
    width = 512
    earlier = (iota((128, 128), 0) < iota((128, 128), 1)).astype(F32).astype(BF16)
    acc_ref[...] = jnp.zeros_like(acc_ref)

    def step(index, counts):
        at = pl.multiple_of(index * width, width)
        band = band_ref[:, pl.ds(at, width)]
        cell = cell_ref[:, pl.ds(at, width)]
        feat = feat_ref[:, pl.ds(at, width)].astype(F32)
        one = (iota((LAT, width), 0) == band).astype(F32)
        ranks = []
        for part in range(width // 128):
            mine = one[:, part * 128 : (part + 1) * 128]
            before = jnp.dot(mine.astype(BF16), earlier, preferred_element_type=F32)
            ranks.append(jnp.sum(mine * (before + counts), axis=0, keepdims=True))
            counts = counts + jnp.sum(mine, axis=1, keepdims=True)
        rank = jnp.concatenate(ranks, axis=1)
        row = lax.shift_right_logical(cell, 11)
        high = lax.bitwise_and(lax.shift_right_logical(cell, 7), 15)
        low = lax.bitwise_and(cell, 127)
        extra = jnp.where(iota((4, width), 0) == 0, row, jnp.where(iota((4, width), 0) == 1, high, low))
        full = jnp.concatenate([feat, extra.astype(F32)], axis=0)
        pieces = [jnp.where(band == which, full, 0.0).astype(BF16) for which in range(LAT)]
        left = jnp.concatenate(pieces, axis=0)
        slot = iota((CAP, width), 0).astype(F32)
        right = jnp.where(slot == rank, 1.0, 0.0).astype(BF16)
        acc_ref[...] += lax.dot_general(left, right, NT, preferred_element_type=F32)
        return counts

    lax.fori_loop(0, ROWS // width, step, jnp.zeros((LAT, 1), F32))
    out_ref[...] = acc_ref[...].reshape(LAT, FEAT, CAP).astype(BF16)


def greet(barrier, axis, me, size):
    def one(step, _):
        pl.semaphore_signal(
            barrier, inc=1, device_id={axis: lax.rem(me + step, size)}, device_id_type=MESH
        )
        return 0

    lax.fori_loop(1, size, one, 0)


def step_offset(step):
    half = (step + 1) // 2
    return lax.rem(jnp.where(lax.rem(step, 2) == 1, half, LAT - half), LAT)


def build_factors(block, lon_ref, col_ref, base):
    feat = block.astype(F32)
    row = feat[12:13].astype(jnp.int32)
    high = feat[13:14].astype(jnp.int32)
    low = feat[14:15].astype(jnp.int32)
    east = lax.bitwise_and(high + 1, 15)
    lane_low = iota((128, CAP), 0)
    first = iota((16, CAP), 0) == 0
    tiles = NLON // 128
    here, there = [
        [
            jnp.broadcast_to(jnp.where(which == tile, 1.0, 0.0), (16, CAP)).astype(BF16)
            for tile in range(tiles)
        ]
        for which in (high, east)
    ]
    for half in range(2):
        west_weight = feat[8 + 2 * half : 9 + 2 * half]
        east_weight = feat[9 + 2 * half : 10 + 2 * half]
        inside = jnp.where(
            lane_low == low, west_weight, jnp.where(lane_low == low + 1, east_weight, 0.0)
        ).astype(BF16)
        across = jnp.where(jnp.logical_and(first, low == 127), east_weight, 0.0).astype(BF16)
        columns = pl.ds(base + half * CAP, CAP)
        head = inside[0:16]
        rest = inside[16:128].reshape(7, 16, CAP)
        for tile in range(tiles):
            lon_ref[pl.ds(tile * 128, 16), columns] = head * here[tile] + across * there[tile]
            lon_ref[pl.ds(tile * 128 + 16, 112), columns] = (rest * here[tile][None]).reshape(112, CAP)
        wanted = iota((LAT, CAP), 0) == row + half
        for channel in range(8):
            value = jnp.where(wanted, feat[channel : channel + 1], 0.0).astype(BF16)
            col_ref[pl.ds(channel * LAT, LAT), columns] = value


def build_blocks(root_ref, block_ref):
    spread = (iota((32, 128), 0) == lax.bitwise_and(iota((32, 128), 1), 31)).astype(F32).astype(BF16)
    group = lax.shift_right_logical(iota((2048, 128), 1), 5)
    for field in range(4):
        copies = jnp.dot(root_ref[field].reshape(2048, 32), spread, preferred_element_type=F32)
        block_ref[:, field * 32 : (field + 1) * 32, :] = (
            jnp.where(group == field, copies, 0.0).astype(BF16).reshape(64, 32, 128)
        )


DEST = 8
GROUP = 4


def grid_kernel(
    band_ref,
    cell_ref,
    feat_ref,
    table_hbm,
    root_hbm,
    dst_ref,
    block_ref,
    packed_ref,
    count_ref,
    recv_ref,
    lon0,
    lon1,
    col0,
    col1,
    grid_ref,
    parts_ref,
    table_ref,
    root_ref,
    src_ref,
    mid_ref,
    row_send,
    row_recv,
    z_send,
    z_recv,
    p_send,
    p_recv,
    own_sem,
):
    me = lax.axis_index("lat")
    lev = lax.axis_index("lev")
    barrier = pltpu.get_barrier_semaphore()
    greet(barrier, "lat", me, LAT)
    greet(barrier, "lev", lev, LEV)
    fetch = pltpu.make_async_copy(table_hbm, table_ref, own_sem.at[0])
    fetch.start()
    fetch_root = pltpu.make_async_copy(root_hbm, root_ref, own_sem.at[1])
    fetch_root.start()
    pack_rows(band_ref, cell_ref, feat_ref, packed_ref, count_ref)
    pl.semaphore_wait(barrier, LAT + LEV - 2)

    def rows(step):
        target = lax.rem(me + step_offset(step), LAT)
        return pltpu.make_async_remote_copy(
            src_ref=packed_ref.at[target],
            dst_ref=recv_ref.at[step],
            send_sem=row_send.at[step],
            recv_sem=row_recv.at[step],
            device_id={"lat": target},
            device_id_type=MESH,
        )

    def start_rows(step, _):
        rows(step).start()
        return 0

    lax.fori_loop(1, LAT, start_rows, 0)
    recv_ref[0] = packed_ref[me]
    grid_ref[...] = jnp.zeros_like(grid_ref)

    def build(step, lon_ref, col_ref):
        for part in range(2):
            build_factors(recv_ref[step + part], lon_ref, col_ref, part * 2 * CAP)

    def add(lon_ref, col_ref):
        for start in range(0, NLON, 1024):
            grid_ref[start : start + 1024] += lax.dot_general(
                lon_ref[start : start + 1024], col_ref[...], NT, preferred_element_type=F32
            )

    rows(1).wait_recv()
    build(0, lon0, col0)

    def scatter(index, _):
        step = 4 * index
        rows(step + 2).wait_recv()
        rows(step + 3).wait_recv()
        build(step + 2, lon1, col1)
        add(lon0, col0)

        @pl.when(index < LAT // 4 - 1)
        def _():
            rows(step + 4).wait_recv()
            rows(step + 5).wait_recv()

        build(lax.rem(step + 4, LAT), lon0, col0)
        add(lon1, col1)
        return 0

    lax.fori_loop(0, LAT // 4, scatter, 0)

    grid = grid_ref[...]
    grid_high = grid.astype(BF16)
    parts_ref[:, 0:256] = grid_high
    parts_ref[:, 256:512] = (grid - grid_high.astype(F32)).astype(BF16)
    fetch.wait()

    def along_lat(target):
        return pltpu.make_async_remote_copy(
            src_ref=src_ref.at[target],
            dst_ref=mid_ref.at[me],
            send_sem=z_send.at[target],
            recv_sem=z_recv.at[me],
            device_id={"lat": target},
            device_id_type=MESH,
        )

    def from_lat(source):
        return pltpu.make_async_remote_copy(
            src_ref=src_ref.at[source],
            dst_ref=mid_ref.at[source],
            send_sem=z_send.at[source],
            recv_sem=z_recv.at[source],
            device_id={"lat": source},
            device_id_type=MESH,
        )

    chunk = DEST * LEV * 4

    def transform(index, _):
        group = lax.rem(me // DEST + index, LAT // DEST)
        at = pl.multiple_of(group * chunk, chunk)
        both = jnp.dot(table_ref[0, pl.ds(at, chunk), :], parts_ref[...], preferred_element_type=F32)
        rest = jnp.dot(
            table_ref[1, pl.ds(at, chunk), :], parts_ref[:, 0:256], preferred_element_type=F32
        )
        total = both[:, 0:256] + both[:, 256:512] + rest
        west = total[:, 0:128].reshape(chunk // 4, 4, 128)
        east = total[:, 128:256].reshape(chunk // 4, 4, 128)
        made = jnp.concatenate([west, east], axis=1).astype(BF16)
        src_ref[pl.ds(group * DEST, DEST)] = made.reshape(DEST, LEV, 8, 128)

        def send(part, _):
            target = group * DEST + part

            @pl.when(target != me)
            def _():
                along_lat(target).start()

            return 0

        lax.fori_loop(0, DEST, send, 0)
        return 0

    lax.fori_loop(0, LAT // DEST, transform, 0)
    mid_ref[me] = src_ref[me]
    fetch_root.wait()
    build_blocks(root_ref, block_ref)

    def along_lev(group, step):
        target = lax.rem(lev + step, LEV)
        places = pl.ds(group * GROUP, GROUP)
        return pltpu.make_async_remote_copy(
            src_ref=mid_ref.at[places, target],
            dst_ref=dst_ref.at[places, lev],
            send_sem=p_send.at[group, step],
            recv_sem=p_recv.at[group, step],
            device_id={"lev": target},
            device_id_type=MESH,
        )

    per = DEST // GROUP

    def forward(index, _):
        band = lax.rem(me // DEST - index // per + LAT // DEST, LAT // DEST)
        group = band * per + lax.rem(index, per)

        def arrive(part, _):
            source = group * GROUP + part

            @pl.when(source != me)
            def _():
                from_lat(source).wait_recv()

            return 0

        lax.fori_loop(0, GROUP, arrive, 0)

        def start_lev(step, _):
            along_lev(group, step).start()
            return 0

        lax.fori_loop(1, LEV, start_lev, 0)
        return 0

    lax.fori_loop(0, LAT // GROUP, forward, 0)
    dst_ref[:, pl.ds(lev, 1)] = mid_ref[:, pl.ds(lev, 1)]

    def sent(step, _):
        rows(step).wait_send()
        along_lat(lax.rem(me + step, LAT)).wait_send()
        return 0

    lax.fori_loop(1, LAT, sent, 0)

    def finish(group, _):
        def one(step, _):
            along_lev(group, step).wait()
            return 0

        lax.fori_loop(1, LEV, one, 0)
        return 0

    lax.fori_loop(0, LAT // GROUP, finish, 0)


def grid_to_pencils(band, cell, feat, table, roots):
    dma = pltpu.SemaphoreType.DMA
    return pl.pallas_call(
        grid_kernel,
        out_shape=[
            jax.ShapeDtypeStruct((LAT, LEV, 8, 128), BF16),
            jax.ShapeDtypeStruct((64, 128, 128), BF16),
        ],
        in_specs=[vmem()] * 3 + [anywhere()] * 2,
        out_specs=[vmem()] * 2,
        scratch_shapes=[
            pltpu.VMEM((LAT, FEAT, CAP), BF16),
            pltpu.VMEM((LAT * FEAT, CAP), F32),
            pltpu.VMEM((LAT, FEAT, CAP), BF16),
            pltpu.VMEM((NLON, 4 * CAP), BF16),
            pltpu.VMEM((NLON, 4 * CAP), BF16),
            pltpu.VMEM((256, 4 * CAP), BF16),
            pltpu.VMEM((256, 4 * CAP), BF16),
            pltpu.VMEM((NLON, 256), F32),
            pltpu.VMEM((NLON, 512), BF16),
            pltpu.VMEM((2, 2 * DEGREES, NLON), BF16),
            pltpu.VMEM((4, 64, 32, 32), BF16),
            pltpu.VMEM((LAT, LEV, 8, 128), BF16),
            pltpu.VMEM((LAT, LEV, 8, 128), BF16),
            dma((LAT,)),
            dma((LAT,)),
            dma((LAT,)),
            dma((LAT,)),
            dma((LAT // GROUP, LEV)),
            dma((LAT // GROUP, LEV)),
            dma((2,)),
        ],
        compiler_params=pltpu.CompilerParams(
            collective_id=0, has_side_effects=True, vmem_limit_bytes=60 << 20
        ),
        name="grid_to_pencils",
    )(band, cell, feat, table, roots)


def spectra_kernel(
    recv_ref,
    table_ref,
    dst_ref,
    out_ref,
    wide_ref,
    order_ref,
    pencil_ref,
    first_ref,
    second_ref,
    send_sem,
    recv_sem,
):
    me = lax.axis_index("lat")
    lev = lax.axis_index("lev")
    pair = me * LEV + lev
    barrier = pltpu.get_barrier_semaphore()
    greet(barrier, "lev", lev, LEV)
    lane = iota((128, 128), 1)
    odd = lax.bitwise_and(lane, 32) != 0
    upper = lane >= 64

    for high in range(8):
        held = []
        for low in range(4):
            held.append(recv_ref[high * 4 + low].reshape(128, 128).astype(F32))
        mixed = [
            jnp.where(odd, pltpu.roll(held[1], 32, 1), held[0]),
            jnp.where(odd, held[1], pltpu.roll(held[0], 96, 1)),
            jnp.where(odd, pltpu.roll(held[3], 32, 1), held[2]),
            jnp.where(odd, held[3], pltpu.roll(held[2], 96, 1)),
        ]
        done = [
            jnp.where(upper, pltpu.roll(mixed[2], 64, 1), mixed[0]),
            jnp.where(upper, pltpu.roll(mixed[3], 64, 1), mixed[1]),
            jnp.where(upper, mixed[2], pltpu.roll(mixed[0], 64, 1)),
            jnp.where(upper, mixed[3], pltpu.roll(mixed[1], 64, 1)),
        ]
        for low in range(4):
            wide_ref[low] = done[low]
        for low in range(4):
            for which in range(4):
                order_ref[pl.ds(which * 128 + low, 32, stride=4), :] = wide_ref[
                    low, pl.ds(which, 32, stride=4), :
                ]
        pencil_ref[:, high * 128 : (high + 1) * 128] = order_ref[...].astype(BF16)

    first_ref[0:DEGREES] = jnp.zeros((DEGREES, 256), F32)
    chunk = 512
    for start in range(0, DEGREES, chunk):
        rows = table_ref[start : start + chunk, :]
        first_ref[DEGREES + start : DEGREES + start + chunk] = lax.dot_general(
            rows, pencil_ref[0:256], NT, preferred_element_type=F32
        )
        second_ref[start : start + chunk] = lax.dot_general(
            rows, pencil_ref[256:512], NT, preferred_element_type=F32
        )
    second_ref[DEGREES : DEGREES + 1] = lax.dot_general(
        table_ref[DEGREES : DEGREES + 1, :], pencil_ref[256:512], NT, preferred_element_type=F32
    )
    begin = [me // 4, LEV - 1 - me // 4]
    pl.semaphore_wait(barrier, LEV - 1)

    def copy(step, slot):
        target = lax.rem(lev + step, LEV)
        return target, pltpu.make_async_remote_copy(
            src_ref=out_ref.at[target, slot],
            dst_ref=dst_ref.at[lev, slot],
            send_sem=send_sem.at[slot, step],
            recv_sem=recv_sem.at[slot, step],
            device_id={"lev": target},
            device_id_type=MESH,
        )

    degree = iota((64, 256), 0)
    skip = lax.rem(8 - lax.rem(pair, 8), 8)

    def start(step, _):
        block = lax.rem(lev + step, LEV)
        base = pl.multiple_of(DEGREES + block * 64 - (pair + 7) // 8 * 8, 8)
        window = first_ref[pl.ds(base, 72), :]
        out_ref[block, 0] = pltpu.roll(window, lax.rem(72 - skip, 72), 0)[0:64].astype(BF16)
        after = second_ref[pl.ds(pl.multiple_of(block * 64, 64), 72), :]
        keep = degree >= DEGREES - 1 - pair - block * 64
        out_ref[block, 1] = jnp.where(keep, pltpu.roll(after, 71, 0)[0:64], 0.0).astype(BF16)
        for slot in range(2):
            target, moving = copy(step, slot)

            @pl.when(jnp.logical_and(step < LEV, target >= begin[slot]))
            def _():
                moving.start()

        return 0

    lax.fori_loop(1, LEV + 1, start, 0)
    dst_ref[lev] = out_ref[lev]

    def clear(step, _):
        source = lax.rem(lev + step, LEV)
        for slot in range(2):

            @pl.when(lev < begin[slot])
            def _():
                dst_ref[source, slot] = jnp.zeros((64, 256), BF16)

        return 0

    lax.fori_loop(1, LEV, clear, 0)

    def finish(step, _):
        for slot in range(2):
            target, moving = copy(step, slot)

            @pl.when(target >= begin[slot])
            def _():
                moving.wait_send()

            @pl.when(lev >= begin[slot])
            def _():
                moving.wait_recv()

        return 0

    lax.fori_loop(1, LEV, finish, 0)


def pencils_to_spectra(received, table):
    dma = pltpu.SemaphoreType.DMA
    return pl.pallas_call(
        spectra_kernel,
        out_shape=jax.ShapeDtypeStruct((LEV, 2, 64, 256), BF16),
        in_specs=[vmem(), vmem()],
        out_specs=vmem(),
        scratch_shapes=[
            pltpu.VMEM((LEV, 2, 64, 256), BF16),
            pltpu.VMEM((4, 128, 128), F32),
            pltpu.VMEM((512, 128), F32),
            pltpu.VMEM((512, NLAT), BF16),
            pltpu.VMEM((2 * DEGREES + 8, 256), F32),
            pltpu.VMEM((DEGREES + 8, 256), F32),
            dma((2, LEV)),
            dma((2, LEV)),
        ],
        compiler_params=pltpu.CompilerParams(
            collective_id=1, has_side_effects=True, vmem_limit_bytes=48 << 20
        ),
        name="pencils_to_spectra",
    )(received, table)


def roots_kernel(spec_ref, block_ref, out_ref, wide_ref):
    for row in range(32):
        block = spec_ref[row // 2, row % 2].astype(F32)
        for part in range(2):
            wide_ref[part, row * 64 : (row + 1) * 64, :] = block[:, part * 128 : (part + 1) * 128]

    def step(degree, _):
        rows = pl.ds(degree, 32, stride=64)
        both = jnp.concatenate([wide_ref[0, rows, :], wide_ref[1, rows, :]], axis=0).astype(BF16)
        made = jnp.dot(both, block_ref[degree], preferred_element_type=F32)
        wide_ref[0, rows, :] = made[0:32]
        wide_ref[1, rows, :] = made[32:64]
        return 0

    lax.fori_loop(0, 64, step, 0, unroll=4)
    for row in range(32):
        lines = pl.ds(row * 64, 64)
        made = jnp.stack([wide_ref[0, lines, :], wide_ref[1, lines, :]], axis=1)
        out_ref[row] = made.astype(BF16)


def apply_roots(blocks, roots):
    return pl.pallas_call(
        roots_kernel,
        out_shape=jax.ShapeDtypeStruct((2 * LEV, 64, 2, 128), BF16),
        in_specs=[vmem(), vmem()],
        out_specs=vmem(),
        scratch_shapes=[pltpu.VMEM((2, 2048, 128), F32)],
        compiler_params=pltpu.CompilerParams(vmem_limit_bytes=48 << 20),
        name="apply_roots",
    )(blocks, roots)


def on_device(table, obs_band, obs_cell, obs_weight, obs_profile, legendre_table, covariance_root):
    feat = jnp.concatenate([obs_profile.T, obs_weight.T], axis=0)
    pencils, root_blocks = grid_to_pencils(
        obs_band.reshape(1, ROWS), obs_cell.reshape(1, ROWS), feat, table, covariance_root
    )
    blocks = pencils_to_spectra(pencils, legendre_table.reshape(DEGREES + 1, NLAT))
    return apply_roots(blocks, root_blocks)


def solution(mesh):
    in_specs = (
        P("lat", None),
        P("lat"),
        P("lat", None),
        P("lat", "lev"),
        P(("lat", "lev"), None, None),
        P(None, "lev", None, None),
    )
    out_specs = P("lat", "lev", None, None)
    table = dft_tables()

    def program(*args):
        return jax.shard_map(
            lambda *inner: on_device(jnp.asarray(table), *inner),
            mesh=mesh,
            in_specs=in_specs,
            out_specs=out_specs,
            check_vma=False,
        )(*args)

    return program
```

```python
import math

import jax
import jax.numpy as jnp
import ml_dtypes
import numpy as np
from jax import lax
from jax.experimental import pallas as pl
from jax.experimental.pallas import tpu as pltpu
from jax.sharding import PartitionSpec as P

NLAT = 1024
NLON = 2048
DEGREES = 1024
LAT = 32
LEV = 16
CAP = 384
ROWS = 4096
FEAT = 16
F32 = jnp.float32
BF16 = jnp.bfloat16
MESH = pl.DeviceIdType.MESH
NT = (((1,), (1,)), ((), ()))


def vmem():
    return pl.BlockSpec(memory_space=pltpu.VMEM)


def anywhere():
    return pl.BlockSpec(memory_space=pl.ANY)


def iota(shape, axis):
    return lax.broadcasted_iota(jnp.int32, shape, axis)


def dft_tables():
    slots = np.arange(DEGREES)
    wave = np.where(slots % 2 == 0, slots // 2, DEGREES - 1 - slots // 2)
    phase = (wave[:, None] * np.arange(NLON)[None, :]) % NLON
    angle = phase * (2.0 * math.pi / NLON)
    table = np.stack([np.cos(angle), -np.sin(angle)], axis=1).reshape(2 * DEGREES, NLON)
    high = table.astype(ml_dtypes.bfloat16)
    low = (table - high.astype(np.float64)).astype(ml_dtypes.bfloat16)
    return np.stack([high, low])


def pack_rows(band_ref, cell_ref, feat_ref, out_ref, acc_ref):
    width = 512
    earlier = (iota((128, 128), 0) < iota((128, 128), 1)).astype(F32).astype(BF16)
    acc_ref[...] = jnp.zeros_like(acc_ref)

    def step(index, counts):
        at = pl.multiple_of(index * width, width)
        band = band_ref[:, pl.ds(at, width)]
        cell = cell_ref[:, pl.ds(at, width)]
        feat = feat_ref[:, pl.ds(at, width)].astype(F32)
        one = (iota((LAT, width), 0) == band).astype(F32)
        ranks = []
        for part in range(width // 128):
            mine = one[:, part * 128 : (part + 1) * 128]
            before = jnp.dot(mine.astype(BF16), earlier, preferred_element_type=F32)
            ranks.append(jnp.sum(mine * (before + counts), axis=0, keepdims=True))
            counts = counts + jnp.sum(mine, axis=1, keepdims=True)
        rank = jnp.concatenate(ranks, axis=1)
        row = lax.shift_right_logical(cell, 11)
        high = lax.bitwise_and(lax.shift_right_logical(cell, 7), 15)
        low = lax.bitwise_and(cell, 127)
        extra = jnp.where(iota((4, width), 0) == 0, row, jnp.where(iota((4, width), 0) == 1, high, low))
        full = jnp.concatenate([feat, extra.astype(F32)], axis=0)
        pieces = [jnp.where(band == which, full, 0.0).astype(BF16) for which in range(LAT)]
        left = jnp.concatenate(pieces, axis=0)
        slot = iota((CAP, width), 0).astype(F32)
        right = jnp.where(slot == rank, 1.0, 0.0).astype(BF16)
        acc_ref[...] += lax.dot_general(left, right, NT, preferred_element_type=F32)
        return counts

    lax.fori_loop(0, ROWS // width, step, jnp.zeros((LAT, 1), F32))
    out_ref[...] = acc_ref[...].reshape(LAT, FEAT, CAP).astype(BF16)


def greet(barrier, axis, me, size):
    def one(step, _):
        pl.semaphore_signal(
            barrier, inc=1, device_id={axis: lax.rem(me + step, size)}, device_id_type=MESH
        )
        return 0

    lax.fori_loop(1, size, one, 0)


def step_offset(step):
    half = (step + 1) // 2
    return lax.rem(jnp.where(lax.rem(step, 2) == 1, half, LAT - half), LAT)


def build_factors(block, half, lon_ref, col_ref, base):
    feat = block.astype(F32)
    row = feat[12:13].astype(jnp.int32)
    high = feat[13:14].astype(jnp.int32)
    low = feat[14:15].astype(jnp.int32)
    columns = pl.ds(base, CAP)
    inside = jnp.where(iota((128, CAP), 0) == low, 1.0, 0.0).astype(BF16).reshape(8, 16, CAP)
    for tile in range(NLON // 128):
        here = jnp.broadcast_to(jnp.where(high == tile, 1.0, 0.0), (16, CAP)).astype(BF16)
        lon_ref[pl.ds(tile * 128, 128), columns] = (inside * here[None]).reshape(128, CAP)
    lat = iota((LAT, CAP), 0)
    south = lat == row
    north = lat == row + 1
    for side in range(2):
        weight = jnp.where(
            south, feat[8 + side : 9 + side], jnp.where(north, feat[10 + side : 11 + side], 0.0)
        )
        for channel in range(4):
            profile = feat[4 * half + channel : 4 * half + channel + 1]
            col_ref[pl.ds(side * 128 + channel * LAT, LAT), columns] = (weight * profile).astype(BF16)


def build_blocks(root_ref, turned_ref, wide_ref, block_ref):
    def turn(field, _):
        for part in range(8):
            piece = root_ref[field, part * 4 : (part + 1) * 4].astype(F32).reshape(128, 64)
            turned_ref[field, part] = jnp.transpose(piece)
        return 0

    lax.fori_loop(0, 4, turn, 0)
    group = lax.shift_right_logical(iota((64, 128), 1), 5)
    for field in range(4):

        def place(part, _):
            piece = turned_ref[field, part]
            for sub in range(4):
                shift = (field - sub) % 4 * 32
                moved = piece if shift == 0 else pltpu.roll(piece, shift, 1)
                rows = pl.ds(field * 32 + part * 4 + sub, 64, stride=128)
                wide_ref[rows, :] = jnp.where(group == field, moved, 0.0)
            return 0

        lax.fori_loop(0, 8, place, 0)
    block_ref[...] = wide_ref[...].reshape(64, 128, 128).astype(BF16)


DEST = 8


def main_kernel(
    band_ref,
    cell_ref,
    feat_ref,
    legendre_ref,
    table_hbm,
    root_hbm,
    spec_ref,
    block_ref,
    packed_ref,
    count_ref,
    recv_ref,
    lon0,
    lon1,
    col0,
    col1,
    grid_ref,
    parts_ref,
    table_ref,
    root_ref,
    turned_ref,
    blocks_ref,
    src_ref,
    mid_ref,
    dst_ref,
    out_ref,
    wide_ref,
    order_ref,
    pencil_ref,
    first_ref,
    second_ref,
    row_send,
    row_recv,
    z_send,
    z_recv,
    p_send,
    p_recv,
    s_send,
    s_recv,
    own_sem,
):
    me = lax.axis_index("lat")
    lev = lax.axis_index("lev")
    pair = me * LEV + lev
    barrier = pltpu.get_barrier_semaphore()
    greet(barrier, "lat", me, LAT)
    greet(barrier, "lev", lev, LEV)
    fetch = pltpu.make_async_copy(table_hbm, table_ref, own_sem.at[0])
    fetch.start()
    fetch_root = pltpu.make_async_copy(root_hbm, root_ref, own_sem.at[1])
    fetch_root.start()
    pack_rows(band_ref, cell_ref, feat_ref, packed_ref, count_ref)
    pl.semaphore_wait(barrier, LAT + LEV - 2)

    def rows(step):
        target = lax.rem(me + step_offset(step), LAT)
        return pltpu.make_async_remote_copy(
            src_ref=packed_ref.at[target],
            dst_ref=recv_ref.at[step],
            send_sem=row_send.at[step],
            recv_sem=row_recv.at[step],
            device_id={"lat": target},
            device_id_type=MESH,
        )

    def start_rows(step, _):
        rows(step).start()
        return 0

    lax.fori_loop(1, LAT, start_rows, 0)
    recv_ref[0] = packed_ref[me]

    def add(lon_ref, col_ref):
        for start in range(0, NLON, 512):
            grid_ref[start : start + 512] += lax.dot_general(
                lon_ref[start : start + 512], col_ref[...], NT, preferred_element_type=F32
            )

    def scatter(half):
        grid_ref[...] = jnp.zeros_like(grid_ref)

        def build(step, lon_ref, col_ref):
            for part in range(2):
                build_factors(recv_ref[step + part], half, lon_ref, col_ref, part * CAP)

        if half == 0:
            rows(1).wait_recv()
        build(0, lon0, col0)

        def step_four(index, _):
            step = 4 * index
            if half == 0:
                rows(step + 2).wait_recv()
                rows(step + 3).wait_recv()
            build(step + 2, lon1, col1)
            add(lon0, col0)
            if half == 0:

                @pl.when(index < LAT // 4 - 1)
                def _():
                    rows(step + 4).wait_recv()
                    rows(step + 5).wait_recv()

            build(lax.rem(step + 4, LAT), lon0, col0)
            add(lon1, col1)
            return 0

        lax.fori_loop(0, LAT // 4, step_four, 0)
        grid = grid_ref[:, 0:128] + pltpu.roll(grid_ref[:, 128:256], 1, 0)
        grid_high = grid.astype(BF16)
        parts_ref[:, 0:128] = grid_high
        parts_ref[:, 128:256] = (grid - grid_high.astype(F32)).astype(BF16)

    def along_lat(half, target):
        return pltpu.make_async_remote_copy(
            src_ref=src_ref.at[half, target],
            dst_ref=mid_ref.at[half, me],
            send_sem=z_send.at[half, target],
            recv_sem=z_recv.at[half, me],
            device_id={"lat": target},
            device_id_type=MESH,
        )

    def from_lat(half, source):
        return pltpu.make_async_remote_copy(
            src_ref=src_ref.at[half, source],
            dst_ref=mid_ref.at[half, source],
            send_sem=z_send.at[half, source],
            recv_sem=z_recv.at[half, source],
            device_id={"lat": source},
            device_id_type=MESH,
        )

    chunk = DEST * LEV * 4
    groups = LAT // DEST

    def transform(half):
        def one(index, _):
            group = lax.rem(me // DEST + index, groups)
            at = pl.multiple_of(group * chunk, chunk)
            both = jnp.dot(table_ref[0, pl.ds(at, chunk), :], parts_ref[...], preferred_element_type=F32)
            rest = jnp.dot(
                table_ref[1, pl.ds(at, chunk), :], parts_ref[:, 0:128], preferred_element_type=F32
            )
            total = both[:, 0:128] + both[:, 128:256] + rest
            src_ref[half, pl.ds(group * DEST, DEST)] = total.reshape(DEST, LEV, 4, 128).astype(BF16)

            def send(part, _):
                target = group * DEST + part

                @pl.when(target != me)
                def _():
                    along_lat(half, target).start()

                return 0

            lax.fori_loop(0, DEST, send, 0)
            return 0

        lax.fori_loop(0, groups, one, 0)
        mid_ref[half, me] = src_ref[half, me]

    def along_lev(half, group, step):
        target = lax.rem(lev + step, LEV)
        places = pl.ds(group * DEST, DEST)
        return pltpu.make_async_remote_copy(
            src_ref=mid_ref.at[half, places, target],
            dst_ref=dst_ref.at[half, places, lev],
            send_sem=p_send.at[half, group, step],
            recv_sem=p_recv.at[half, group, step],
            device_id={"lev": target},
            device_id_type=MESH,
        )

    def forward(half):
        def one(index, _):
            group = lax.rem(me // DEST - index + groups, groups)

            def arrive(part, _):
                source = group * DEST + part

                @pl.when(source != me)
                def _():
                    from_lat(half, source).wait_recv()

                return 0

            lax.fori_loop(0, DEST, arrive, 0)

            def start_lev(step, _):
                along_lev(half, group, step).start()
                return 0

            lax.fori_loop(1, LEV, start_lev, 0)
            return 0

        lax.fori_loop(0, groups, one, 0)
        dst_ref[half, :, pl.ds(lev, 1)] = mid_ref[half, :, pl.ds(lev, 1)]

    def arrived(half):
        def one(index, _):
            along_lev(half, index // (LEV - 1), 1 + lax.rem(index, LEV - 1)).wait_recv()
            return 0

        lax.fori_loop(0, groups * (LEV - 1), one, 0)

    lane = iota((64, 128), 1)
    odd = lax.bitwise_and(lane, 32) != 0
    upper = lane >= 64

    def turn(half):
        for high in range(8):
            held = [dst_ref[half, high * 4 + low].astype(F32).reshape(64, 128) for low in range(4)]
            mixed = [
                jnp.where(odd, pltpu.roll(held[1], 32, 1), held[0]),
                jnp.where(odd, held[1], pltpu.roll(held[0], 96, 1)),
                jnp.where(odd, pltpu.roll(held[3], 32, 1), held[2]),
                jnp.where(odd, held[3], pltpu.roll(held[2], 96, 1)),
            ]
            done = [
                jnp.where(upper, pltpu.roll(mixed[2], 64, 1), mixed[0]),
                jnp.where(upper, pltpu.roll(mixed[3], 64, 1), mixed[1]),
                jnp.where(upper, mixed[2], pltpu.roll(mixed[0], 64, 1)),
                jnp.where(upper, mixed[3], pltpu.roll(mixed[1], 64, 1)),
            ]
            for low in range(4):
                wide_ref[low] = done[low]
            for low in range(4):
                for which in range(4):
                    place = pl.ds(which * 128 + half * 4 + low, 16, stride=8)
                    order_ref[high, place, :] = wide_ref[low, pl.ds(which, 16, stride=4), :]

    scatter(0)
    fetch.wait()
    transform(0)
    scatter(1)
    transform(1)
    forward(0)
    fetch_root.wait()
    build_blocks(root_ref, turned_ref, blocks_ref, block_ref)
    arrived(0)
    turn(0)
    forward(1)
    arrived(1)
    turn(1)
    for high in range(8):
        pencil_ref[:, high * 128 : (high + 1) * 128] = order_ref[high].astype(BF16)

    first_ref[0:DEGREES] = jnp.zeros((DEGREES, 256), F32)
    size = 512
    for start in range(0, DEGREES, size):
        lines = legendre_ref[start : start + size, :]
        first_ref[DEGREES + start : DEGREES + start + size] = lax.dot_general(
            lines, pencil_ref[0:256], NT, preferred_element_type=F32
        )
        second_ref[start : start + size] = lax.dot_general(
            lines, pencil_ref[256:512], NT, preferred_element_type=F32
        )
    second_ref[DEGREES : DEGREES + 1] = lax.dot_general(
        legendre_ref[DEGREES : DEGREES + 1, :], pencil_ref[256:512], NT, preferred_element_type=F32
    )

    begin = [me // 4, LEV - 1 - me // 4]

    def spectra(step, slot):
        target = lax.rem(lev + step, LEV)
        return target, pltpu.make_async_remote_copy(
            src_ref=out_ref.at[target, slot],
            dst_ref=spec_ref.at[lev, slot],
            send_sem=s_send.at[slot, step],
            recv_sem=s_recv.at[slot, step],
            device_id={"lev": target},
            device_id_type=MESH,
        )

    degree = iota((64, 256), 0)
    skip = lax.rem(8 - lax.rem(pair, 8), 8)

    def start_spectra(step, _):
        block = lax.rem(lev + step, LEV)
        base = pl.multiple_of(DEGREES + block * 64 - (pair + 7) // 8 * 8, 8)
        window = first_ref[pl.ds(base, 72), :]
        out_ref[block, 0] = pltpu.roll(window, lax.rem(72 - skip, 72), 0)[0:64].astype(BF16)
        after = second_ref[pl.ds(pl.multiple_of(block * 64, 64), 72), :]
        keep = degree >= DEGREES - 1 - pair - block * 64
        out_ref[block, 1] = jnp.where(keep, pltpu.roll(after, 71, 0)[0:64], 0.0).astype(BF16)
        for slot in range(2):
            target, moving = spectra(step, slot)

            @pl.when(jnp.logical_and(step < LEV, target >= begin[slot]))
            def _():
                moving.start()

        return 0

    lax.fori_loop(1, LEV + 1, start_spectra, 0)
    spec_ref[lev] = out_ref[lev]

    def clear(step, _):
        source = lax.rem(lev + step, LEV)
        for slot in range(2):

            @pl.when(lev < begin[slot])
            def _():
                spec_ref[source, slot] = jnp.zeros((64, 256), BF16)

        return 0

    lax.fori_loop(1, LEV, clear, 0)

    def sent(step, _):
        rows(step).wait_send()
        for half in range(2):
            along_lat(half, lax.rem(me + step, LAT)).wait_send()
        return 0

    lax.fori_loop(1, LAT, sent, 0)

    def finish(step, _):
        for half in range(2):
            for group in range(groups):
                along_lev(half, group, step).wait_send()
        for slot in range(2):
            target, moving = spectra(step, slot)

            @pl.when(target >= begin[slot])
            def _():
                moving.wait_send()

            @pl.when(lev >= begin[slot])
            def _():
                moving.wait_recv()

        return 0

    lax.fori_loop(1, LEV, finish, 0)


def rows_to_spectra(band, cell, feat, legendre_table, table, roots):
    dma = pltpu.SemaphoreType.DMA
    return pl.pallas_call(
        main_kernel,
        out_shape=[
            jax.ShapeDtypeStruct((LEV, 2, 64, 256), BF16),
            jax.ShapeDtypeStruct((64, 128, 128), BF16),
        ],
        in_specs=[vmem()] * 4 + [anywhere()] * 2,
        out_specs=[vmem()] * 2,
        scratch_shapes=[
            pltpu.VMEM((LAT, FEAT, CAP), BF16),
            pltpu.VMEM((LAT * FEAT, CAP), F32),
            pltpu.VMEM((LAT, FEAT, CAP), BF16),
            pltpu.VMEM((NLON, 2 * CAP), BF16),
            pltpu.VMEM((NLON, 2 * CAP), BF16),
            pltpu.VMEM((256, 2 * CAP), BF16),
            pltpu.VMEM((256, 2 * CAP), BF16),
            pltpu.VMEM((NLON, 256), F32),
            pltpu.VMEM((NLON, 256), BF16),
            pltpu.VMEM((2, 2 * DEGREES, NLON), BF16),
            pltpu.VMEM((4, 32, 32, 64), BF16),
            pltpu.VMEM((4, 8, 64, 128), F32),
            pltpu.VMEM((64 * 128, 128), F32),
            pltpu.VMEM((2, LAT, LEV, 4, 128), BF16),
            pltpu.VMEM((2, LAT, LEV, 4, 128), BF16),
            pltpu.VMEM((2, LAT, LEV, 4, 128), BF16),
            pltpu.VMEM((LEV, 2, 64, 256), BF16),
            pltpu.VMEM((4, 64, 128), F32),
            pltpu.VMEM((8, 512, 128), F32),
            pltpu.VMEM((512, NLAT), BF16),
            pltpu.VMEM((2 * DEGREES + 8, 256), F32),
            pltpu.VMEM((DEGREES + 8, 256), F32),
            dma((LAT,)),
            dma((LAT,)),
            dma((2, LAT)),
            dma((2, LAT)),
            dma((2, LAT // DEST, LEV)),
            dma((2, LAT // DEST, LEV)),
            dma((2, LEV)),
            dma((2, LEV)),
            dma((2,)),
        ],
        compiler_params=pltpu.CompilerParams(
            collective_id=0, has_side_effects=True, vmem_limit_bytes=60 << 20
        ),
        name="rows_to_spectra",
    )(band, cell, feat, legendre_table, table, roots)


def roots_kernel(spec_ref, block_ref, out_ref, wide_ref, made_ref):
    for row in range(32):
        block = spec_ref[row // 2, row % 2].astype(F32)
        for part in range(2):
            wide_ref[part, row * 64 : (row + 1) * 64, :] = block[:, part * 128 : (part + 1) * 128]

    def step(degree, _):
        rows = pl.ds(degree, 32, stride=64)
        both = jnp.concatenate([wide_ref[0, rows, :], wide_ref[1, rows, :]], axis=0).astype(BF16)
        made = jnp.dot(both, block_ref[degree], preferred_element_type=F32)
        made_ref[0, rows, :] = made[0:32]
        made_ref[1, rows, :] = made[32:64]
        return 0

    lax.fori_loop(0, 64, step, 0, unroll=8)
    for row in range(32):
        lines = pl.ds(row * 64, 64)
        made = jnp.stack([made_ref[0, lines, :], made_ref[1, lines, :]], axis=1)
        out_ref[row] = made.astype(BF16)


def apply_roots(blocks, roots):
    return pl.pallas_call(
        roots_kernel,
        out_shape=jax.ShapeDtypeStruct((2 * LEV, 64, 2, 128), BF16),
        in_specs=[vmem(), vmem()],
        out_specs=vmem(),
        scratch_shapes=[pltpu.VMEM((2, 2048, 128), F32), pltpu.VMEM((2, 2048, 128), F32)],
        compiler_params=pltpu.CompilerParams(vmem_limit_bytes=48 << 20),
        name="apply_roots",
    )(blocks, roots)


def on_device(table, obs_band, obs_cell, obs_weight, obs_profile, legendre_table, covariance_root):
    feat = jnp.concatenate([obs_profile.T, obs_weight.T], axis=0)
    blocks, root_blocks = rows_to_spectra(
        obs_band.reshape(1, ROWS),
        obs_cell.reshape(1, ROWS),
        feat,
        legendre_table.reshape(DEGREES + 1, NLAT),
        table,
        jnp.transpose(covariance_root, (0, 2, 3, 1)),
    )
    return apply_roots(blocks, root_blocks)


def solution(mesh):
    in_specs = (
        P("lat", None),
        P("lat"),
        P("lat", None),
        P("lat", "lev"),
        P(("lat", "lev"), None, None),
        P(None, "lev", None, None),
    )
    out_specs = P("lat", "lev", None, None)
    table = dft_tables()

    def program(*args):
        return jax.shard_map(
            lambda *inner: on_device(jnp.asarray(table), *inner),
            mesh=mesh,
            in_specs=in_specs,
            out_specs=out_specs,
            check_vma=False,
        )(*args)

    return program
```

```python
import math

import jax
import jax.numpy as jnp
import ml_dtypes
import numpy as np
from jax import lax
from jax.experimental import pallas as pl
from jax.experimental.pallas import tpu as pltpu
from jax.sharding import PartitionSpec as P

NLAT = 1024
NLON = 2048
DEGREES = 1024
LAT = 32
LEV = 16
CAP = 384
ROWS = 4096
FEAT = 16
F32 = jnp.float32
BF16 = jnp.bfloat16
MESH = pl.DeviceIdType.MESH
NT = (((1,), (1,)), ((), ()))


def vmem():
    return pl.BlockSpec(memory_space=pltpu.VMEM)


def anywhere():
    return pl.BlockSpec(memory_space=pl.ANY)


def iota(shape, axis):
    return lax.broadcasted_iota(jnp.int32, shape, axis)


def dft_tables():
    slots = np.arange(DEGREES)
    wave = np.where(slots % 2 == 0, slots // 2, DEGREES - 1 - slots // 2)
    phase = (wave[:, None] * np.arange(NLON)[None, :]) % NLON
    angle = phase * (2.0 * math.pi / NLON)
    table = np.stack([np.cos(angle), -np.sin(angle)], axis=1).reshape(2 * DEGREES, NLON)
    high = table.astype(ml_dtypes.bfloat16)
    low = (table - high.astype(np.float64)).astype(ml_dtypes.bfloat16)
    return np.stack([high, low])


def pack_rows(band_ref, cell_ref, profile_ref, weight_ref, out_ref, acc_ref):
    width = 512
    earlier = (iota((128, 128), 0) < iota((128, 128), 1)).astype(F32).astype(BF16)
    acc_ref[...] = jnp.zeros_like(acc_ref)

    def step(index, counts):
        at = pl.multiple_of(index * width, width)
        band = band_ref[:, pl.ds(at, width)]
        cell = cell_ref[:, pl.ds(at, width)]
        profile = profile_ref[:, pl.ds(at, width)].astype(F32)
        weight = weight_ref[:, pl.ds(at, width)].astype(F32)
        one = (iota((LAT, width), 0) == band).astype(F32)
        ranks = []
        for part in range(width // 128):
            mine = one[:, part * 128 : (part + 1) * 128]
            before = jnp.dot(mine.astype(BF16), earlier, preferred_element_type=F32)
            ranks.append(jnp.sum(mine * (before + counts), axis=0, keepdims=True))
            counts = counts + jnp.sum(mine, axis=1, keepdims=True)
        rank = jnp.concatenate(ranks, axis=1)
        row = lax.shift_right_logical(cell, 11)
        high = lax.bitwise_and(lax.shift_right_logical(cell, 7), 15)
        low = lax.bitwise_and(cell, 127)
        extra = jnp.where(iota((4, width), 0) == 0, row, jnp.where(iota((4, width), 0) == 1, high, low))
        full = jnp.concatenate([profile, weight, extra.astype(F32)], axis=0)
        pieces = [jnp.where(band == which, full, 0.0).astype(BF16) for which in range(LAT)]
        left = jnp.concatenate(pieces, axis=0)
        slot = iota((CAP, width), 0).astype(F32)
        right = jnp.where(slot == rank, 1.0, 0.0).astype(BF16)
        acc_ref[...] += lax.dot_general(left, right, NT, preferred_element_type=F32)
        return counts

    lax.fori_loop(0, ROWS // width, step, jnp.zeros((LAT, 1), F32))
    out_ref[...] = acc_ref[...].reshape(LAT, FEAT, CAP).astype(BF16)


def greet(barrier, axis, me, size):
    def one(step, _):
        pl.semaphore_signal(
            barrier, inc=1, device_id={axis: lax.rem(me + step, size)}, device_id_type=MESH
        )
        return 0

    lax.fori_loop(1, size, one, 0)


def step_offset(step):
    half = (step + 1) // 2
    return lax.rem(jnp.where(lax.rem(step, 2) == 1, half, LAT - half), LAT)


def build_factors(block, half, lon_ref, col_ref, base):
    feat = block.astype(F32)
    row = feat[12:13].astype(jnp.int32)
    high = feat[13:14].astype(jnp.int32)
    low = feat[14:15].astype(jnp.int32)
    columns = pl.ds(base, CAP)
    inside = jnp.where(iota((128, CAP), 0) == low, 1.0, 0.0).astype(BF16).reshape(8, 16, CAP)
    for tile in range(NLON // 128):
        here = jnp.broadcast_to(jnp.where(high == tile, 1.0, 0.0), (16, CAP)).astype(BF16)
        lon_ref[pl.ds(tile * 128, 128), columns] = (inside * here[None]).reshape(128, CAP)
    lat = iota((LAT, CAP), 0)
    south = lat == row
    north = lat == row + 1
    for side in range(2):
        weight = jnp.where(
            south, feat[8 + side : 9 + side], jnp.where(north, feat[10 + side : 11 + side], 0.0)
        )
        for channel in range(4):
            profile = feat[4 * half + channel : 4 * half + channel + 1]
            col_ref[pl.ds(side * 128 + channel * LAT, LAT), columns] = (weight * profile).astype(BF16)


def build_blocks(root_ref, turned_ref, wide_ref, block_ref):
    def turn(field, _):
        for part in range(8):
            piece = root_ref[field, part * 4 : (part + 1) * 4].astype(F32).reshape(128, 64)
            turned_ref[field, part] = jnp.transpose(piece)
        return 0

    lax.fori_loop(0, 4, turn, 0)
    group = lax.shift_right_logical(iota((64, 128), 1), 5)
    for field in range(4):

        def place(part, _):
            piece = turned_ref[field, part]
            for sub in range(4):
                shift = (field - sub) % 4 * 32
                moved = piece if shift == 0 else pltpu.roll(piece, shift, 1)
                rows = pl.ds(field * 32 + part * 4 + sub, 64, stride=128)
                wide_ref[rows, :] = jnp.where(group == field, moved, 0.0)
            return 0

        lax.fori_loop(0, 8, place, 0)
    block_ref[...] = wide_ref[...].reshape(64, 128, 128).astype(BF16)


DEST = 8


def main_kernel(
    band_ref,
    cell_ref,
    profile_ref,
    weight_ref,
    legendre_ref,
    table_hbm,
    root_hbm,
    spec_ref,
    block_ref,
    packed_ref,
    count_ref,
    recv_ref,
    lon0,
    lon1,
    col0,
    col1,
    grid_ref,
    parts_ref,
    table_ref,
    root_ref,
    turned_ref,
    blocks_ref,
    src_ref,
    mid_ref,
    dst_ref,
    out_ref,
    wide_ref,
    order_ref,
    pencil_ref,
    first_ref,
    second_ref,
    row_send,
    row_recv,
    z_send,
    z_recv,
    p_send,
    p_recv,
    s_send,
    s_recv,
    own_sem,
):
    me = lax.axis_index("lat")
    lev = lax.axis_index("lev")
    pair = me * LEV + lev
    barrier = pltpu.get_barrier_semaphore()
    greet(barrier, "lat", me, LAT)
    greet(barrier, "lev", lev, LEV)
    fetch = pltpu.make_async_copy(table_hbm, table_ref, own_sem.at[0])
    fetch.start()
    fetch_root = pltpu.make_async_copy(root_hbm, root_ref, own_sem.at[1])
    fetch_root.start()
    pack_rows(band_ref, cell_ref, profile_ref, weight_ref, packed_ref, count_ref)
    pl.semaphore_wait(barrier, LAT + LEV - 2)

    def rows(step):
        target = lax.rem(me + step_offset(step), LAT)
        return pltpu.make_async_remote_copy(
            src_ref=packed_ref.at[target],
            dst_ref=recv_ref.at[step],
            send_sem=row_send.at[step],
            recv_sem=row_recv.at[step],
            device_id={"lat": target},
            device_id_type=MESH,
        )

    def start_rows(step, _):
        rows(step).start()
        return 0

    lax.fori_loop(1, LAT, start_rows, 0)
    recv_ref[0] = packed_ref[me]

    def add(lon_ref, col_ref):
        for start in range(0, NLON, 512):
            grid_ref[start : start + 512] += lax.dot_general(
                lon_ref[start : start + 512], col_ref[...], NT, preferred_element_type=F32
            )

    def scatter(half):
        grid_ref[...] = jnp.zeros_like(grid_ref)

        def build(step, lon_ref, col_ref):
            for part in range(2):
                build_factors(recv_ref[step + part], half, lon_ref, col_ref, part * CAP)

        if half == 0:
            rows(1).wait_recv()
        build(0, lon0, col0)

        def step_four(index, _):
            step = 4 * index
            if half == 0:
                rows(step + 2).wait_recv()
                rows(step + 3).wait_recv()
            build(step + 2, lon1, col1)
            add(lon0, col0)
            if half == 0:

                @pl.when(index < LAT // 4 - 1)
                def _():
                    rows(step + 4).wait_recv()
                    rows(step + 5).wait_recv()

            build(lax.rem(step + 4, LAT), lon0, col0)
            add(lon1, col1)
            return 0

        lax.fori_loop(0, LAT // 4, step_four, 0)
        grid = grid_ref[:, 0:128] + pltpu.roll(grid_ref[:, 128:256], 1, 0)
        grid_high = grid.astype(BF16)
        parts_ref[:, 0:128] = grid_high
        parts_ref[:, 128:256] = (grid - grid_high.astype(F32)).astype(BF16)

    def along_lat(half, target):
        return pltpu.make_async_remote_copy(
            src_ref=src_ref.at[half, target],
            dst_ref=mid_ref.at[half, me],
            send_sem=z_send.at[half, target],
            recv_sem=z_recv.at[half, me],
            device_id={"lat": target},
            device_id_type=MESH,
        )

    def from_lat(half, source):
        return pltpu.make_async_remote_copy(
            src_ref=src_ref.at[half, source],
            dst_ref=mid_ref.at[half, source],
            send_sem=z_send.at[half, source],
            recv_sem=z_recv.at[half, source],
            device_id={"lat": source},
            device_id_type=MESH,
        )

    chunk = DEST * LEV * 4
    groups = LAT // DEST

    def transform(half):
        def one(index, _):
            group = lax.rem(me // DEST + index, groups)
            at = pl.multiple_of(group * chunk, chunk)
            both = jnp.dot(table_ref[0, pl.ds(at, chunk), :], parts_ref[...], preferred_element_type=F32)
            rest = jnp.dot(
                table_ref[1, pl.ds(at, chunk), :], parts_ref[:, 0:128], preferred_element_type=F32
            )
            total = both[:, 0:128] + both[:, 128:256] + rest
            src_ref[half, pl.ds(group * DEST, DEST)] = total.reshape(DEST, LEV, 4, 128).astype(BF16)

            def send(part, _):
                target = group * DEST + part

                @pl.when(target != me)
                def _():
                    along_lat(half, target).start()

                return 0

            lax.fori_loop(0, DEST, send, 0)
            return 0

        lax.fori_loop(0, groups, one, 0)
        mid_ref[half, me] = src_ref[half, me]

    def along_lev(half, group, step):
        target = lax.rem(lev + step, LEV)
        places = pl.ds(group * DEST, DEST)
        return pltpu.make_async_remote_copy(
            src_ref=mid_ref.at[half, places, target],
            dst_ref=dst_ref.at[half, places, lev],
            send_sem=p_send.at[half, group, step],
            recv_sem=p_recv.at[half, group, step],
            device_id={"lev": target},
            device_id_type=MESH,
        )

    def forward(half):
        def one(index, _):
            group = lax.rem(me // DEST - index + groups, groups)

            def arrive(part, _):
                source = group * DEST + part

                @pl.when(source != me)
                def _():
                    from_lat(half, source).wait_recv()

                return 0

            lax.fori_loop(0, DEST, arrive, 0)

            def start_lev(step, _):
                along_lev(half, group, step).start()
                return 0

            lax.fori_loop(1, LEV, start_lev, 0)
            return 0

        lax.fori_loop(0, groups, one, 0)
        dst_ref[half, :, pl.ds(lev, 1)] = mid_ref[half, :, pl.ds(lev, 1)]

    def arrived(half):
        def one(index, _):
            along_lev(half, index // (LEV - 1), 1 + lax.rem(index, LEV - 1)).wait_recv()
            return 0

        lax.fori_loop(0, groups * (LEV - 1), one, 0)

    lane = iota((64, 128), 1)
    odd = lax.bitwise_and(lane, 32) != 0
    upper = lane >= 64

    def turn(half):
        for high in range(8):
            held = [dst_ref[half, high * 4 + low].astype(F32).reshape(64, 128) for low in range(4)]
            mixed = [
                jnp.where(odd, pltpu.roll(held[1], 32, 1), held[0]),
                jnp.where(odd, held[1], pltpu.roll(held[0], 96, 1)),
                jnp.where(odd, pltpu.roll(held[3], 32, 1), held[2]),
                jnp.where(odd, held[3], pltpu.roll(held[2], 96, 1)),
            ]
            done = [
                jnp.where(upper, pltpu.roll(mixed[2], 64, 1), mixed[0]),
                jnp.where(upper, pltpu.roll(mixed[3], 64, 1), mixed[1]),
                jnp.where(upper, mixed[2], pltpu.roll(mixed[0], 64, 1)),
                jnp.where(upper, mixed[3], pltpu.roll(mixed[1], 64, 1)),
            ]
            for low in range(4):
                wide_ref[low] = done[low]
            for low in range(4):
                for which in range(4):
                    place = pl.ds(which * 128 + half * 4 + low, 16, stride=8)
                    order_ref[high, place, :] = wide_ref[low, pl.ds(which, 16, stride=4), :]

    scatter(0)
    fetch.wait()
    transform(0)
    scatter(1)
    transform(1)
    forward(0)
    fetch_root.wait()
    build_blocks(root_ref, turned_ref, blocks_ref, block_ref)
    first_ref[0:DEGREES] = jnp.zeros((DEGREES, 256), F32)
    second_ref[0 : DEGREES // 2] = jnp.zeros((DEGREES // 2, 256), F32)
    arrived(0)
    turn(0)
    forward(1)
    arrived(1)
    turn(1)
    for high in range(8):
        pencil_ref[:, high * 128 : (high + 1) * 128] = order_ref[high].astype(BF16)

    size = 512
    for start in range(0, DEGREES, size):
        lines = legendre_ref[start : start + size, :]
        first_ref[DEGREES + start : DEGREES + start + size] = lax.dot_general(
            lines, pencil_ref[0:256], NT, preferred_element_type=F32
        )
        if start >= DEGREES // 2:
            second_ref[start : start + size] = lax.dot_general(
                lines, pencil_ref[256:512], NT, preferred_element_type=F32
            )
    second_ref[DEGREES : DEGREES + 1] = lax.dot_general(
        legendre_ref[DEGREES : DEGREES + 1, :], pencil_ref[256:512], NT, preferred_element_type=F32
    )

    begin = [me // 4, LEV - 1 - me // 4]

    def spectra(step, slot):
        target = lax.rem(lev + step, LEV)
        return target, pltpu.make_async_remote_copy(
            src_ref=out_ref.at[target, slot],
            dst_ref=spec_ref.at[lev, slot],
            send_sem=s_send.at[slot, step],
            recv_sem=s_recv.at[slot, step],
            device_id={"lev": target},
            device_id_type=MESH,
        )

    degree = iota((64, 256), 0)
    skip = lax.rem(8 - lax.rem(pair, 8), 8)

    def start_spectra(step, _):
        block = lax.rem(lev + step, LEV)
        base = pl.multiple_of(DEGREES + block * 64 - (pair + 7) // 8 * 8, 8)
        window = first_ref[pl.ds(base, 72), :]
        out_ref[block, 0] = pltpu.roll(window, lax.rem(72 - skip, 72), 0)[0:64].astype(BF16)
        after = second_ref[pl.ds(pl.multiple_of(block * 64, 64), 72), :]
        keep = degree >= DEGREES - 1 - pair - block * 64
        out_ref[block, 1] = jnp.where(keep, pltpu.roll(after, 71, 0)[0:64], 0.0).astype(BF16)
        for slot in range(2):
            target, moving = spectra(step, slot)

            @pl.when(jnp.logical_and(step < LEV, target >= begin[slot]))
            def _():
                moving.start()

        return 0

    lax.fori_loop(1, LEV + 1, start_spectra, 0)
    spec_ref[lev] = out_ref[lev]

    def clear(step, _):
        source = lax.rem(lev + step, LEV)
        for slot in range(2):

            @pl.when(lev < begin[slot])
            def _():
                spec_ref[source, slot] = jnp.zeros((64, 256), BF16)

        return 0

    lax.fori_loop(1, LEV, clear, 0)

    def sent(step, _):
        rows(step).wait_send()
        for half in range(2):
            along_lat(half, lax.rem(me + step, LAT)).wait_send()
        return 0

    lax.fori_loop(1, LAT, sent, 0)

    def finish(step, _):
        for half in range(2):
            for group in range(groups):
                along_lev(half, group, step).wait_send()
        for slot in range(2):
            target, moving = spectra(step, slot)

            @pl.when(target >= begin[slot])
            def _():
                moving.wait_send()

            @pl.when(lev >= begin[slot])
            def _():
                moving.wait_recv()

        return 0

    lax.fori_loop(1, LEV, finish, 0)


def rows_to_spectra(band, cell, profile, weight, legendre_table, table, roots):
    dma = pltpu.SemaphoreType.DMA
    return pl.pallas_call(
        main_kernel,
        out_shape=[
            jax.ShapeDtypeStruct((LEV, 2, 64, 256), BF16),
            jax.ShapeDtypeStruct((64, 128, 128), BF16),
        ],
        in_specs=[vmem()] * 5 + [anywhere()] * 2,
        out_specs=[vmem()] * 2,
        scratch_shapes=[
            pltpu.VMEM((LAT, FEAT, CAP), BF16),
            pltpu.VMEM((LAT * FEAT, CAP), F32),
            pltpu.VMEM((LAT, FEAT, CAP), BF16),
            pltpu.VMEM((NLON, 2 * CAP), BF16),
            pltpu.VMEM((NLON, 2 * CAP), BF16),
            pltpu.VMEM((256, 2 * CAP), BF16),
            pltpu.VMEM((256, 2 * CAP), BF16),
            pltpu.VMEM((NLON, 256), F32),
            pltpu.VMEM((NLON, 256), BF16),
            pltpu.VMEM((2, 2 * DEGREES, NLON), BF16),
            pltpu.VMEM((4, 32, 32, 64), BF16),
            pltpu.VMEM((4, 8, 64, 128), F32),
            pltpu.VMEM((64 * 128, 128), F32),
            pltpu.VMEM((2, LAT, LEV, 4, 128), BF16),
            pltpu.VMEM((2, LAT, LEV, 4, 128), BF16),
            pltpu.VMEM((2, LAT, LEV, 4, 128), BF16),
            pltpu.VMEM((LEV, 2, 64, 256), BF16),
            pltpu.VMEM((4, 64, 128), F32),
            pltpu.VMEM((8, 512, 128), F32),
            pltpu.VMEM((512, NLAT), BF16),
            pltpu.VMEM((2 * DEGREES + 8, 256), F32),
            pltpu.VMEM((DEGREES + 8, 256), F32),
            dma((LAT,)),
            dma((LAT,)),
            dma((2, LAT)),
            dma((2, LAT)),
            dma((2, LAT // DEST, LEV)),
            dma((2, LAT // DEST, LEV)),
            dma((2, LEV)),
            dma((2, LEV)),
            dma((2,)),
        ],
        compiler_params=pltpu.CompilerParams(
            collective_id=0, has_side_effects=True, vmem_limit_bytes=46 << 20
        ),
        name="rows_to_spectra",
    )(band, cell, profile, weight, legendre_table, table, roots)


STRIDE = 72
WIDE = 136


def roots_kernel(spec_ref, block_ref, out_ref, wide_ref, made_ref):
    for row in range(32):
        block = spec_ref[row // 2, row % 2].astype(F32)
        for part in range(2):
            wide_ref[part, row * STRIDE : row * STRIDE + 64, :] = block[:, part * 128 : (part + 1) * 128]

    def step(degree, _):
        rows = pl.ds(degree, 32, stride=STRIDE)
        both = jnp.concatenate([wide_ref[0, rows, :], wide_ref[1, rows, :]], axis=0).astype(BF16)
        made = jnp.dot(both, block_ref[degree], preferred_element_type=F32)
        for part in range(2):
            place = pl.ds(2 * degree + part, 32, stride=WIDE)
            made_ref[place, :] = made[part * 32 : (part + 1) * 32]
        return 0

    lax.fori_loop(0, 64, step, 0, unroll=8)
    for row in range(32):
        out_ref[row] = made_ref[row * WIDE : row * WIDE + 128, :].astype(BF16)


def apply_roots(blocks, roots):
    return pl.pallas_call(
        roots_kernel,
        out_shape=jax.ShapeDtypeStruct((2 * LEV, 128, 128), BF16),
        in_specs=[vmem(), vmem()],
        out_specs=vmem(),
        scratch_shapes=[
            pltpu.VMEM((2, 32 * STRIDE, 128), F32),
            pltpu.VMEM((32 * WIDE, 128), F32),
        ],
        compiler_params=pltpu.CompilerParams(vmem_limit_bytes=48 << 20),
        name="apply_roots",
    )(blocks, roots)


def on_device(table, obs_band, obs_cell, obs_weight, obs_profile, legendre_table, covariance_root):
    blocks, root_blocks = rows_to_spectra(
        obs_band.reshape(1, ROWS),
        obs_cell.reshape(1, ROWS),
        obs_profile.T,
        obs_weight.T,
        legendre_table.reshape(DEGREES + 1, NLAT),
        table,
        jnp.transpose(covariance_root, (0, 2, 3, 1)),
    )
    return apply_roots(blocks, root_blocks).reshape(2 * LEV, 64, 2, 128)


def solution(mesh):
    in_specs = (
        P("lat", None),
        P("lat"),
        P("lat", None),
        P("lat", "lev"),
        P(("lat", "lev"), None, None),
        P(None, "lev", None, None),
    )
    out_specs = P("lat", "lev", None, None)
    table = dft_tables()

    def program(*args):
        return jax.shard_map(
            lambda *inner: on_device(jnp.asarray(table), *inner),
            mesh=mesh,
            in_specs=in_specs,
            out_specs=out_specs,
            check_vma=False,
        )(*args)

    return program
```

```python
import math

import jax
import jax.numpy as jnp
import ml_dtypes
import numpy as np
from jax import lax
from jax.experimental import pallas as pl
from jax.experimental.pallas import tpu as pltpu
from jax.sharding import PartitionSpec as P

NLAT = 1024
NLON = 2048
DEGREES = 1024
LAT = 32
LEV = 16
CAP = 384
ROWS = 4096
FEAT = 16
F32 = jnp.float32
BF16 = jnp.bfloat16
MESH = pl.DeviceIdType.MESH
NT = (((1,), (1,)), ((), ()))


def vmem():
    return pl.BlockSpec(memory_space=pltpu.VMEM)


def outside():
    return pl.BlockSpec(memory_space=pltpu.HBM)


def iota(shape, axis):
    return lax.broadcasted_iota(jnp.int32, shape, axis)


def dft_tables():
    slots = np.arange(DEGREES)
    wave = np.where(slots % 2 == 0, slots // 2, DEGREES - 1 - slots // 2)
    phase = (wave[:, None] * np.arange(NLON)[None, :]) % NLON
    angle = phase * (2.0 * math.pi / NLON)
    table = np.stack([np.cos(angle), -np.sin(angle)], axis=1).reshape(2 * DEGREES, NLON)
    high = table.astype(ml_dtypes.bfloat16)
    low = (table - high.astype(np.float64)).astype(ml_dtypes.bfloat16)
    return np.stack([high, low])


def pack_rows(band_ref, cell_ref, profile_ref, weight_ref, out_ref, acc_ref):
    width = 512
    earlier = (iota((128, 128), 0) < iota((128, 128), 1)).astype(F32).astype(BF16)
    acc_ref[...] = jnp.zeros_like(acc_ref)

    def step(index, counts):
        at = pl.multiple_of(index * width, width)
        band = band_ref[:, pl.ds(at, width)]
        cell = cell_ref[:, pl.ds(at, width)]
        profile = profile_ref[:, pl.ds(at, width)].astype(F32)
        weight = weight_ref[:, pl.ds(at, width)].astype(F32)
        one = (iota((LAT, width), 0) == band).astype(F32)
        ranks = []
        for part in range(width // 128):
            mine = one[:, part * 128 : (part + 1) * 128]
            before = jnp.dot(mine.astype(BF16), earlier, preferred_element_type=F32)
            ranks.append(jnp.sum(mine * (before + counts), axis=0, keepdims=True))
            counts = counts + jnp.sum(mine, axis=1, keepdims=True)
        rank = jnp.concatenate(ranks, axis=1)
        row = lax.shift_right_logical(cell, 11)
        high = lax.bitwise_and(lax.shift_right_logical(cell, 7), 15)
        low = lax.bitwise_and(cell, 127)
        extra = jnp.where(iota((4, width), 0) == 0, row, jnp.where(iota((4, width), 0) == 1, high, low))
        full = jnp.concatenate([profile, weight, extra.astype(F32)], axis=0)
        pieces = [jnp.where(band == which, full, 0.0).astype(BF16) for which in range(LAT)]
        left = jnp.concatenate(pieces, axis=0)
        slot = iota((CAP, width), 0).astype(F32)
        right = jnp.where(slot == rank, 1.0, 0.0).astype(BF16)
        acc_ref[...] += lax.dot_general(left, right, NT, preferred_element_type=F32)
        return counts

    lax.fori_loop(0, ROWS // width, step, jnp.zeros((LAT, 1), F32))
    out_ref[...] = acc_ref[...].reshape(LAT, FEAT, CAP).astype(BF16)


def greet(barrier, axis, me, size):
    def one(step, _):
        pl.semaphore_signal(
            barrier, inc=1, device_id={axis: lax.rem(me + step, size)}, device_id_type=MESH
        )
        return 0

    lax.fori_loop(1, size, one, 0)


def step_offset(step):
    half = (step + 1) // 2
    return lax.rem(jnp.where(lax.rem(step, 2) == 1, half, LAT - half), LAT)


def build_factors(block, half, lon_ref, col_ref, base):
    feat = block.astype(F32)
    row = feat[12:13].astype(jnp.int32)
    high = feat[13:14].astype(jnp.int32)
    low = feat[14:15].astype(jnp.int32)
    columns = pl.ds(base, CAP)
    inside = jnp.where(iota((128, CAP), 0) == low, 1.0, 0.0).astype(BF16).reshape(8, 16, CAP)
    for tile in range(NLON // 128):
        here = jnp.broadcast_to(jnp.where(high == tile, 1.0, 0.0), (16, CAP)).astype(BF16)
        lon_ref[pl.ds(tile * 128, 128), columns] = (inside * here[None]).reshape(128, CAP)
    lat = iota((LAT, CAP), 0)
    south = lat == row
    north = lat == row + 1
    for side in range(2):
        weight = jnp.where(
            south, feat[8 + side : 9 + side], jnp.where(north, feat[10 + side : 11 + side], 0.0)
        )
        for channel in range(4):
            profile = feat[4 * half + channel : 4 * half + channel + 1]
            col_ref[pl.ds(side * 128 + channel * LAT, LAT), columns] = (weight * profile).astype(BF16)


def build_blocks(root_ref, turned_ref, wide_ref, block_ref):
    def turn(field, _):
        for part in range(8):
            piece = root_ref[field, part * 4 : (part + 1) * 4].astype(F32).reshape(128, 64)
            turned_ref[field, part] = jnp.transpose(piece)
        return 0

    lax.fori_loop(0, 4, turn, 0)
    group = lax.shift_right_logical(iota((64, 128), 1), 5)
    for field in range(4):

        def place(part, _):
            piece = turned_ref[field, part]
            for sub in range(4):
                shift = (field - sub) % 4 * 32
                moved = piece if shift == 0 else pltpu.roll(piece, shift, 1)
                rows = pl.ds(field * 32 + part * 4 + sub, 64, stride=128)
                wide_ref[rows, :] = jnp.where(group == field, moved, 0.0)
            return 0

        lax.fori_loop(0, 8, place, 0)
    block_ref[...] = wide_ref[...].reshape(64, 128, 128).astype(BF16)


DEST = 8


def main_kernel(
    band_hbm,
    cell_hbm,
    profile_hbm,
    weight_hbm,
    legendre_hbm,
    table_hbm,
    root_hbm,
    spec_ref,
    block_ref,
    packed_ref,
    count_ref,
    recv_ref,
    lon0,
    lon1,
    col0,
    col1,
    grid_ref,
    parts_ref,
    table_ref,
    root_ref,
    turned_ref,
    blocks_ref,
    src_ref,
    mid_ref,
    dst_ref,
    out_ref,
    wide_ref,
    order_ref,
    pencil_ref,
    first_ref,
    second_ref,
    band_ref,
    cell_ref,
    profile_ref,
    weight_ref,
    legendre_ref,
    row_send,
    row_recv,
    z_send,
    z_recv,
    p_send,
    p_recv,
    s_send,
    s_recv,
    own_sem,
):
    me = lax.axis_index("lat")
    lev = lax.axis_index("lev")
    pair = me * LEV + lev
    barrier = pltpu.get_barrier_semaphore()
    inputs = [
        pltpu.make_async_copy(band_hbm, band_ref, own_sem.at[2]),
        pltpu.make_async_copy(cell_hbm, cell_ref, own_sem.at[3]),
        pltpu.make_async_copy(profile_hbm, profile_ref, own_sem.at[4]),
        pltpu.make_async_copy(weight_hbm, weight_ref, own_sem.at[5]),
    ]
    for moving in inputs:
        moving.start()
    greet(barrier, "lat", me, LAT)
    greet(barrier, "lev", lev, LEV)
    fetch_legendre = pltpu.make_async_copy(legendre_hbm, legendre_ref, own_sem.at[6])
    for moving in inputs:
        moving.wait()
    fetch = pltpu.make_async_copy(table_hbm, table_ref, own_sem.at[0])
    fetch.start()
    fetch_root = pltpu.make_async_copy(root_hbm, root_ref, own_sem.at[1])
    fetch_root.start()
    fetch_legendre.start()
    pack_rows(band_ref, cell_ref, profile_ref, weight_ref, packed_ref, count_ref)
    pl.semaphore_wait(barrier, LAT + LEV - 2)

    def rows(step):
        target = lax.rem(me + step_offset(step), LAT)
        return pltpu.make_async_remote_copy(
            src_ref=packed_ref.at[target],
            dst_ref=recv_ref.at[step],
            send_sem=row_send.at[step],
            recv_sem=row_recv.at[step],
            device_id={"lat": target},
            device_id_type=MESH,
        )

    def start_rows(step, _):
        rows(step).start()
        return 0

    lax.fori_loop(1, LAT, start_rows, 0)
    recv_ref[0] = packed_ref[me]

    def add(lon_ref, col_ref):
        for start in range(0, NLON, 512):
            grid_ref[start : start + 512] += lax.dot_general(
                lon_ref[start : start + 512], col_ref[...], NT, preferred_element_type=F32
            )

    def scatter(half):
        grid_ref[...] = jnp.zeros_like(grid_ref)

        def build(step, lon_ref, col_ref):
            for part in range(2):
                build_factors(recv_ref[step + part], half, lon_ref, col_ref, part * CAP)

        if half == 0:
            rows(1).wait_recv()
        build(0, lon0, col0)

        def step_four(index, _):
            step = 4 * index
            if half == 0:
                rows(step + 2).wait_recv()
                rows(step + 3).wait_recv()
            build(step + 2, lon1, col1)
            add(lon0, col0)
            if half == 0:

                @pl.when(index < LAT // 4 - 1)
                def _():
                    rows(step + 4).wait_recv()
                    rows(step + 5).wait_recv()

            build(lax.rem(step + 4, LAT), lon0, col0)
            add(lon1, col1)
            return 0

        lax.fori_loop(0, LAT // 4, step_four, 0)
        grid = grid_ref[:, 0:128] + pltpu.roll(grid_ref[:, 128:256], 1, 0)
        grid_high = grid.astype(BF16)
        parts_ref[:, 0:128] = grid_high
        parts_ref[:, 128:256] = (grid - grid_high.astype(F32)).astype(BF16)

    def along_lat(half, target):
        return pltpu.make_async_remote_copy(
            src_ref=src_ref.at[half, target],
            dst_ref=mid_ref.at[half, me],
            send_sem=z_send.at[half, target],
            recv_sem=z_recv.at[half, me],
            device_id={"lat": target},
            device_id_type=MESH,
        )

    def from_lat(half, source):
        return pltpu.make_async_remote_copy(
            src_ref=src_ref.at[half, source],
            dst_ref=mid_ref.at[half, source],
            send_sem=z_send.at[half, source],
            recv_sem=z_recv.at[half, source],
            device_id={"lat": source},
            device_id_type=MESH,
        )

    chunk = DEST * LEV * 4
    groups = LAT // DEST

    def transform(half):
        def one(index, _):
            group = lax.rem(me // DEST + index, groups)
            at = pl.multiple_of(group * chunk, chunk)
            both = jnp.dot(table_ref[0, pl.ds(at, chunk), :], parts_ref[...], preferred_element_type=F32)
            rest = jnp.dot(
                table_ref[1, pl.ds(at, chunk), :], parts_ref[:, 0:128], preferred_element_type=F32
            )
            total = both[:, 0:128] + both[:, 128:256] + rest
            src_ref[half, pl.ds(group * DEST, DEST)] = total.reshape(DEST, LEV, 4, 128).astype(BF16)

            def send(part, _):
                target = group * DEST + part

                @pl.when(target != me)
                def _():
                    along_lat(half, target).start()

                return 0

            lax.fori_loop(0, DEST, send, 0)
            return 0

        lax.fori_loop(0, groups, one, 0)
        mid_ref[half, me] = src_ref[half, me]

    def along_lev(half, group, step):
        target = lax.rem(lev + step, LEV)
        places = pl.ds(group * DEST, DEST)
        return pltpu.make_async_remote_copy(
            src_ref=mid_ref.at[half, places, target],
            dst_ref=dst_ref.at[half, places, lev],
            send_sem=p_send.at[half, group, step],
            recv_sem=p_recv.at[half, group, step],
            device_id={"lev": target},
            device_id_type=MESH,
        )

    def forward(half):
        def one(index, _):
            group = lax.rem(me // DEST - index + groups, groups)

            def arrive(part, _):
                source = group * DEST + part

                @pl.when(source != me)
                def _():
                    from_lat(half, source).wait_recv()

                return 0

            lax.fori_loop(0, DEST, arrive, 0)

            def start_lev(step, _):
                along_lev(half, group, step).start()
                return 0

            lax.fori_loop(1, LEV, start_lev, 0)
            return 0

        lax.fori_loop(0, groups, one, 0)
        dst_ref[half, :, pl.ds(lev, 1)] = mid_ref[half, :, pl.ds(lev, 1)]

    def arrived(half):
        def one(index, _):
            along_lev(half, index // (LEV - 1), 1 + lax.rem(index, LEV - 1)).wait_recv()
            return 0

        lax.fori_loop(0, groups * (LEV - 1), one, 0)

    lane = iota((64, 128), 1)
    odd = lax.bitwise_and(lane, 32) != 0
    upper = lane >= 64

    def turn(half):
        for high in range(8):
            held = [dst_ref[half, high * 4 + low].astype(F32).reshape(64, 128) for low in range(4)]
            mixed = [
                jnp.where(odd, pltpu.roll(held[1], 32, 1), held[0]),
                jnp.where(odd, held[1], pltpu.roll(held[0], 96, 1)),
                jnp.where(odd, pltpu.roll(held[3], 32, 1), held[2]),
                jnp.where(odd, held[3], pltpu.roll(held[2], 96, 1)),
            ]
            done = [
                jnp.where(upper, pltpu.roll(mixed[2], 64, 1), mixed[0]),
                jnp.where(upper, pltpu.roll(mixed[3], 64, 1), mixed[1]),
                jnp.where(upper, mixed[2], pltpu.roll(mixed[0], 64, 1)),
                jnp.where(upper, mixed[3], pltpu.roll(mixed[1], 64, 1)),
            ]
            for low in range(4):
                wide_ref[low] = done[low]
            for low in range(4):
                for which in range(4):
                    place = pl.ds(which * 128 + half * 4 + low, 16, stride=8)
                    order_ref[high, place, :] = wide_ref[low, pl.ds(which, 16, stride=4), :]

    scatter(0)
    fetch.wait()
    transform(0)
    scatter(1)
    transform(1)
    forward(0)
    fetch_root.wait()
    fetch_legendre.wait()
    build_blocks(root_ref, turned_ref, blocks_ref, block_ref)
    first_ref[0:DEGREES] = jnp.zeros((DEGREES, 256), F32)
    second_ref[0 : DEGREES // 2] = jnp.zeros((DEGREES // 2, 256), F32)
    arrived(0)
    turn(0)
    forward(1)
    arrived(1)
    turn(1)
    for high in range(8):
        pencil_ref[:, high * 128 : (high + 1) * 128] = order_ref[high].astype(BF16)

    size = 512
    for start in range(0, DEGREES, size):
        lines = legendre_ref[start : start + size, :]
        first_ref[DEGREES + start : DEGREES + start + size] = lax.dot_general(
            lines, pencil_ref[0:256], NT, preferred_element_type=F32
        )
        if start >= DEGREES // 2:
            second_ref[start : start + size] = lax.dot_general(
                lines, pencil_ref[256:512], NT, preferred_element_type=F32
            )
    second_ref[DEGREES : DEGREES + 1] = lax.dot_general(
        legendre_ref[DEGREES : DEGREES + 1, :], pencil_ref[256:512], NT, preferred_element_type=F32
    )

    begin = [me // 4, LEV - 1 - me // 4]

    def spectra(step, slot):
        target = lax.rem(lev + step, LEV)
        return target, pltpu.make_async_remote_copy(
            src_ref=out_ref.at[target, slot],
            dst_ref=spec_ref.at[lev, slot],
            send_sem=s_send.at[slot, step],
            recv_sem=s_recv.at[slot, step],
            device_id={"lev": target},
            device_id_type=MESH,
        )

    degree = iota((64, 256), 0)
    skip = lax.rem(8 - lax.rem(pair, 8), 8)

    def start_spectra(step, _):
        block = lax.rem(lev + step, LEV)
        base = pl.multiple_of(DEGREES + block * 64 - (pair + 7) // 8 * 8, 8)
        window = first_ref[pl.ds(base, 72), :]
        out_ref[block, 0] = pltpu.roll(window, lax.rem(72 - skip, 72), 0)[0:64].astype(BF16)
        after = second_ref[pl.ds(pl.multiple_of(block * 64, 64), 72), :]
        keep = degree >= DEGREES - 1 - pair - block * 64
        out_ref[block, 1] = jnp.where(keep, pltpu.roll(after, 71, 0)[0:64], 0.0).astype(BF16)
        for slot in range(2):
            target, moving = spectra(step, slot)

            @pl.when(jnp.logical_and(step < LEV, target >= begin[slot]))
            def _():
                moving.start()

        return 0

    lax.fori_loop(1, LEV + 1, start_spectra, 0)
    spec_ref[lev] = out_ref[lev]

    def clear(step, _):
        source = lax.rem(lev + step, LEV)
        for slot in range(2):

            @pl.when(lev < begin[slot])
            def _():
                spec_ref[source, slot] = jnp.zeros((64, 256), BF16)

        return 0

    lax.fori_loop(1, LEV, clear, 0)

    def sent(step, _):
        rows(step).wait_send()
        for half in range(2):
            along_lat(half, lax.rem(me + step, LAT)).wait_send()
        return 0

    lax.fori_loop(1, LAT, sent, 0)

    def finish(step, _):
        for half in range(2):
            for group in range(groups):
                along_lev(half, group, step).wait_send()
        for slot in range(2):
            target, moving = spectra(step, slot)

            @pl.when(target >= begin[slot])
            def _():
                moving.wait_send()

            @pl.when(lev >= begin[slot])
            def _():
                moving.wait_recv()

        return 0

    lax.fori_loop(1, LEV, finish, 0)


def rows_to_spectra(band, cell, profile, weight, legendre_table, table, roots):
    dma = pltpu.SemaphoreType.DMA
    return pl.pallas_call(
        main_kernel,
        out_shape=[
            jax.ShapeDtypeStruct((LEV, 2, 64, 256), BF16),
            jax.ShapeDtypeStruct((64, 128, 128), BF16),
        ],
        in_specs=[outside()] * 7,
        out_specs=[vmem()] * 2,
        scratch_shapes=[
            pltpu.VMEM((LAT, FEAT, CAP), BF16),
            pltpu.VMEM((LAT * FEAT, CAP), F32),
            pltpu.VMEM((LAT, FEAT, CAP), BF16),
            pltpu.VMEM((NLON, 2 * CAP), BF16),
            pltpu.VMEM((NLON, 2 * CAP), BF16),
            pltpu.VMEM((256, 2 * CAP), BF16),
            pltpu.VMEM((256, 2 * CAP), BF16),
            pltpu.VMEM((NLON, 256), F32),
            pltpu.VMEM((NLON, 256), BF16),
            pltpu.VMEM((2, 2 * DEGREES, NLON), BF16),
            pltpu.VMEM((4, 32, 32, 64), BF16),
            pltpu.VMEM((4, 8, 64, 128), F32),
            pltpu.VMEM((64 * 128, 128), F32),
            pltpu.VMEM((2, LAT, LEV, 4, 128), BF16),
            pltpu.VMEM((2, LAT, LEV, 4, 128), BF16),
            pltpu.VMEM((2, LAT, LEV, 4, 128), BF16),
            pltpu.VMEM((LEV, 2, 64, 256), BF16),
            pltpu.VMEM((4, 64, 128), F32),
            pltpu.VMEM((8, 512, 128), F32),
            pltpu.VMEM((512, NLAT), BF16),
            pltpu.VMEM((2 * DEGREES + 8, 256), F32),
            pltpu.VMEM((DEGREES + 8, 256), F32),
            pltpu.VMEM((1, ROWS), jnp.int32),
            pltpu.VMEM((1, ROWS), jnp.int32),
            pltpu.VMEM((8, ROWS), BF16),
            pltpu.VMEM((4, ROWS), BF16),
            pltpu.VMEM((DEGREES + 1, NLAT), BF16),
            dma((LAT,)),
            dma((LAT,)),
            dma((2, LAT)),
            dma((2, LAT)),
            dma((2, LAT // DEST, LEV)),
            dma((2, LAT // DEST, LEV)),
            dma((2, LEV)),
            dma((2, LEV)),
            dma((7,)),
        ],
        compiler_params=pltpu.CompilerParams(
            collective_id=0, has_side_effects=True, vmem_limit_bytes=48 << 20
        ),
        name="rows_to_spectra",
    )(band, cell, profile, weight, legendre_table, table, roots)


STRIDE = 72
WIDE = 136


def roots_kernel(spec_ref, block_ref, out_ref, wide_ref, made_ref):
    for row in range(32):
        block = spec_ref[row // 2, row % 2].astype(F32)
        for part in range(2):
            wide_ref[part, row * STRIDE : row * STRIDE + 64, :] = block[:, part * 128 : (part + 1) * 128]

    def step(degree, _):
        rows = pl.ds(degree, 32, stride=STRIDE)
        both = jnp.concatenate([wide_ref[0, rows, :], wide_ref[1, rows, :]], axis=0).astype(BF16)
        made = jnp.dot(both, block_ref[degree], preferred_element_type=F32)
        for part in range(2):
            place = pl.ds(2 * degree + part, 32, stride=WIDE)
            made_ref[place, :] = made[part * 32 : (part + 1) * 32]
        return 0

    lax.fori_loop(0, 64, step, 0, unroll=8)
    for row in range(32):
        out_ref[row] = made_ref[row * WIDE : row * WIDE + 128, :].astype(BF16)


def apply_roots(blocks, roots):
    return pl.pallas_call(
        roots_kernel,
        out_shape=jax.ShapeDtypeStruct((2 * LEV, 128, 128), BF16),
        in_specs=[vmem(), vmem()],
        out_specs=vmem(),
        scratch_shapes=[
            pltpu.VMEM((2, 32 * STRIDE, 128), F32),
            pltpu.VMEM((32 * WIDE, 128), F32),
        ],
        compiler_params=pltpu.CompilerParams(vmem_limit_bytes=48 << 20),
        name="apply_roots",
    )(blocks, roots)


def on_device(table, obs_band, obs_cell, obs_weight, obs_profile, legendre_table, covariance_root):
    blocks, root_blocks = rows_to_spectra(
        obs_band.reshape(1, ROWS),
        obs_cell.reshape(1, ROWS),
        obs_profile.T,
        obs_weight.T,
        legendre_table.reshape(DEGREES + 1, NLAT),
        table,
        jnp.transpose(covariance_root, (0, 2, 3, 1)),
    )
    return apply_roots(blocks, root_blocks).reshape(2 * LEV, 64, 2, 128)


def solution(mesh):
    in_specs = (
        P("lat", None),
        P("lat"),
        P("lat", None),
        P("lat", "lev"),
        P(("lat", "lev"), None, None),
        P(None, "lev", None, None),
    )
    out_specs = P("lat", "lev", None, None)
    table = dft_tables()

    def program(*args):
        return jax.shard_map(
            lambda *inner: on_device(jnp.asarray(table), *inner),
            mesh=mesh,
            in_specs=in_specs,
            out_specs=out_specs,
            check_vma=False,
        )(*args)

    return program
```
